256 devices in a mesh: graph: 64 (over x, z, core), slab: 4 (over y).
Axes of the slice: x: 4, y: 4, z: 8, core: 2. Of those that a mesh axis runs over, the one named last changes fastest.
Arguments:
- feats: bfloat16 [64, 4, 256, 256], P('graph', 'slab'), may hold values from -6 to 6
- w_self: bfloat16 [256, 256], replicated, may hold values from -0.375 to 0.375
- w_neigh: bfloat16 [256, 256], replicated, may hold values from -0.375 to 0.375
- block_vals: bfloat16 [64, 4, 32, 128, 128], P('graph', 'slab'), may hold values from -0.125 to 0.125
- block_dst: int32 [64, 4, 32], P('graph', 'slab'), may hold values from 0 to 1
- block_src: int32 [64, 4, 32], P('graph', 'slab'), may hold values from 0 to 7
- block_count: int32 [64, 4], P('graph', 'slab'), may hold values from 8 to 32, as said below
- prev_partial: bfloat16 [64, 4, 256, 256], P('graph', 'slab'), may hold values from -6 to 6
- mirror_rows: int32 [64, 4, 64, 4], P('graph', 'slab'), may hold values from 0 to 255, as said below
- send_count: int32 [64, 4, 64], P('graph', 'slab'), may hold values from 0 to 4, as said below
- master_rows: int32 [64, 4, 64, 4], P('graph', 'slab'), may hold values from 0 to 255
- momentum: float32 [64, 4, 256, 256], P('graph', 'slab'), may hold values from -6 to 6
- cotangent: bfloat16 [64, 4, 256, 256], P('graph', 'slab'), may hold values from -6 to 6
- prev_grad: bfloat16 [64, 4, 256, 256], P('graph', 'slab'), may hold values from -6 to 6
- grad_momentum: float32 [64, 4, 256, 256], P('graph', 'slab'), may hold values from -6 to 6
Outputs:
- hidden: bfloat16 [64, 4, 256, 256], P('graph', 'slab')
- feat_grad: bfloat16 [64, 4, 256, 256], P('graph', 'slab')
- smoothed_partials: float32 [64, 4, 256, 256], P('graph', 'slab')
- smoothed_grads: float32 [64, 4, 256, 256], P('graph', 'slab')
- w_grads: float32 [2, 256, 256], replicated
The draws below stay inside these ranges and needn't reach their ends.
Inputs may be any that keep to these rules, and one draw needn't show every extreme that they name: `block_count`: blocks at positions at or past the count are ignored; some device has all 32 live in every draw. `mirror_rows`: rows are distinct over all peers and slots of one device. `send_count`: slots at or past the count are ignored; a device's count for its own partition is 0; every device has 4 for some peer.
All inputs are finite; a program needn't handle non-finite values.
Results may differ from the reference program's by a relative error of at most 0.022.
The reference program's roundings to bfloat16 on the way (of `agg`, `delta` and `grad_agg`) count: a program that leaves them out, or rounds other values in their place, can miss the bound.
Values may be sent and summed in bfloat16 or wider, within the bound.
A program may use at most 64 MiB of HBM per device.

```python
import jax
import jax.numpy as jnp
from jax import lax

F = 256
BLK = 128
BPR = 16
R = 256
NB = 32
CAP = 4
SRC_TILES = 8
ALL_ROWS = 65536
N_GRAPH = 64
N_SLAB = 4


def draw_block_count(key, part):
    key = jax.random.fold_in(key, 11)
    first, second = jax.random.split(key)
    counts = jax.random.randint(first, (N_GRAPH * N_SLAB,), NB // 4, NB + 1)
    place = jax.random.randint(second, (), 0, N_GRAPH * N_SLAB)
    counts = jnp.where(jnp.arange(N_GRAPH * N_SLAB) == place, NB, counts)
    return counts.reshape(N_GRAPH, N_SLAB).astype(jnp.int32)


def draw_mirror_rows(key, part):
    key = jax.random.fold_in(key, 23)
    keys = jax.random.split(key, N_GRAPH * N_SLAB)
    rows = jax.vmap(lambda one: jax.random.permutation(one, R)[:N_GRAPH * CAP])(keys)
    return rows.reshape(N_GRAPH, N_SLAB, N_GRAPH, CAP).astype(jnp.int32)


def draw_send_count(key, part):
    key = jax.random.fold_in(key, 37)
    first, second = jax.random.split(key)
    counts = jax.random.randint(first, (N_GRAPH, N_SLAB, N_GRAPH), 1, CAP + 1)
    offset = jax.random.randint(second, (N_GRAPH, N_SLAB), 1, N_GRAPH)
    own = jnp.arange(N_GRAPH)[:, None]
    target = (own + offset) % N_GRAPH
    peers = jnp.arange(N_GRAPH)[None, None, :]
    counts = jnp.where(peers == target[..., None], CAP, counts)
    counts = jnp.where(peers == jnp.arange(N_GRAPH)[:, None, None], 0, counts)
    return counts.astype(jnp.int32)


def with_ends(values, rng, smallest, high):
    longest = values.shape.index(max(values.shape))
    spots = []
    for shift in (0, 1):
        where = [jax.random.randint(jax.random.fold_in(rng, axis), (), 0, length) for axis, length in enumerate(values.shape)]
        where[longest] = (where[longest] + shift) % values.shape[longest]
        spots.append(tuple(where))
    return values.at[spots[0]].set(smallest).at[spots[1]].set(high)


def levels(rng, shape, cuts, least, high):
    def one(position, parts):
        steps = jax.random.uniform(jax.random.fold_in(jax.random.fold_in(rng, 6), position), (parts,), jnp.float32, least / len(cuts), high / len(cuts))
        return jnp.repeat(jnp.exp(steps), shape[position] // parts).reshape((-1,) + (1,) * (len(shape) - position - 1))

    level = one(*cuts[0])
    for cut in cuts[1:]:
        level = level * one(*cut)
    return level


def gaussian(key, dims, scale, most, cuts=(), kind=jnp.bfloat16):
    array = scale * jax.random.normal(key, dims, jnp.float32)
    if cuts:
        array = array * levels(key, dims, cuts, -0.22, 0.18)
    return jnp.clip(array, -most, most).astype(kind)


def setup_inputs(seed: int = 0) -> dict:
    splits = jax.random.split(jax.random.key(seed), 16)
    return {
        "feats": gaussian(splits[0], (N_GRAPH, N_SLAB, R, F), 1.0, 6.0, ((0, 64), (1, 4))),
        "w_self": gaussian(splits[1], (F, F), F ** -0.5, 0.375),
        "w_neigh": gaussian(splits[2], (F, F), F ** -0.5, 0.375),
        "block_vals": gaussian(splits[3], (N_GRAPH, N_SLAB, NB, BLK, BLK), (BPR * BLK) ** -0.5, 0.125, ((0, 64), (1, 4))),
        "block_dst": with_ends(jax.random.randint(splits[4], (N_GRAPH, N_SLAB, NB), 0, R // BLK), jax.random.fold_in(splits[4], 1), 0, (R // BLK) - 1).astype(jnp.int32),
        "block_src": with_ends(jax.random.randint(splits[5], (N_GRAPH, N_SLAB, NB), 0, SRC_TILES), jax.random.fold_in(splits[5], 1), 0, SRC_TILES - 1).astype(jnp.int32),
        "block_count": draw_block_count(jax.random.fold_in(splits[15], 71), 0),
        "prev_partial": gaussian(splits[7], (N_GRAPH, N_SLAB, R, F), 1.0, 6.0, ((0, 64), (1, 4))),
        "mirror_rows": draw_mirror_rows(jax.random.fold_in(splits[15], 71), 0),
        "send_count": draw_send_count(jax.random.fold_in(splits[15], 71), 0),
        "master_rows": with_ends(jax.random.randint(splits[10], (N_GRAPH, N_SLAB, N_GRAPH, CAP), 0, R), jax.random.fold_in(splits[10], 1), 0, R - 1).astype(jnp.int32),
        "momentum": gaussian(splits[11], (N_GRAPH, N_SLAB, R, F), 1.0, 6.0, ((0, 64), (1, 4)), jnp.float32),
        "cotangent": gaussian(splits[12], (N_GRAPH, N_SLAB, R, F), 1.0, 6.0, ((0, 64), (1, 4))),
        "prev_grad": gaussian(splits[13], (N_GRAPH, N_SLAB, R, F), 1.0, 6.0, ((0, 64), (1, 4))),
        "grad_momentum": gaussian(splits[14], (N_GRAPH, N_SLAB, R, F), 1.0, 6.0, ((0, 64), (1, 4)), jnp.float32),
    }


SMOOTHING = 0.7

def pick_rows(table, rows):
    return table[rows]

def add_rows(values, rows):
    width = values.shape[-1]
    start = jnp.zeros((R, width), jnp.float32)
    return start.at[rows.reshape(-1)].add(values.reshape(-1, width))

def reference(feats, w_self, w_neigh, block_vals, block_dst, block_src, block_count, prev_partial, mirror_rows, send_count, master_rows, momentum, cotangent, prev_grad, grad_momentum):
    slot = jnp.arange(CAP, dtype=jnp.int32)
    live_slot = slot[None, None, None, :] < send_count[..., None]
    sent = jax.vmap(jax.vmap(pick_rows))(prev_partial, mirror_rows).astype(jnp.float32)
    sent = jnp.where(live_slot[..., None], sent, 0.0)
    arrived = jnp.transpose(sent, (2, 1, 0, 3, 4))
    boundary = jax.vmap(jax.vmap(add_rows))(arrived, master_rows)
    smoothed_partials = SMOOTHING * momentum + (1.0 - SMOOTHING) * boundary
    back = jax.vmap(jax.vmap(pick_rows))(prev_grad, master_rows).astype(jnp.float32)
    back = jnp.transpose(back, (2, 1, 0, 3, 4))
    back = jnp.where(live_slot[..., None], back, 0.0)
    returned = jax.vmap(jax.vmap(add_rows))(back, mirror_rows)
    smoothed_grads = SMOOTHING * grad_momentum + (1.0 - SMOOTHING) * returned

    def one_partition(index):
        group_tiles = feats[index].reshape(SRC_TILES, BLK, F).astype(jnp.float32)
        outputs = []
        grads_self = []
        grads_neigh = []
        src_total = jnp.zeros((N_SLAB * R, F), jnp.float32)
        for slab in range(N_SLAB):
            vals = block_vals[index, slab].astype(jnp.float32)
            dst = block_dst[index, slab]
            src = block_src[index, slab]
            live = jnp.arange(NB, dtype=jnp.int32) < block_count[index, slab]
            tiles = group_tiles[src]
            prods = jnp.einsum('bij,bjf->bif', vals, tiles, precision=lax.Precision.HIGHEST)
            prods = jnp.where(live[:, None, None], prods, 0.0)
            local = jax.ops.segment_sum(prods, dst, num_segments=R // BLK).reshape(R, F)
            agg = (local + smoothed_partials[index, slab]).astype(jnp.bfloat16)
            own = feats[index, slab]
            pre = jnp.dot(own, w_self, preferred_element_type=jnp.float32) + jnp.dot(agg, w_neigh, preferred_element_type=jnp.float32)
            out = jnp.maximum(pre, 0.0).astype(jnp.bfloat16)
            delta = jnp.where(pre > 0, cotangent[index, slab], jnp.zeros_like(cotangent[index, slab]))
            grads_self.append(jnp.dot(own.T, delta, preferred_element_type=jnp.float32))
            grads_neigh.append(jnp.dot(agg.T, delta, preferred_element_type=jnp.float32))
            grad_agg = (jnp.dot(delta, w_neigh.T, preferred_element_type=jnp.float32) + smoothed_grads[index, slab]).astype(jnp.bfloat16)
            dtiles = grad_agg.reshape(R // BLK, BLK, F).astype(jnp.float32)[dst]
            backs = jnp.einsum('bji,bjf->bif', vals, dtiles, precision=lax.Precision.HIGHEST)
            backs = jnp.where(live[:, None, None], backs, 0.0)
            src_total = src_total + jax.ops.segment_sum(backs, src, num_segments=SRC_TILES).reshape(N_SLAB * R, F)
            self_part = jnp.dot(delta, w_self.T, preferred_element_type=jnp.float32)
            outputs.append((out, self_part))
        hid = jnp.stack([pair[0] for pair in outputs])
        selfs = jnp.stack([pair[1] for pair in outputs])
        fgrad = (selfs + src_total.reshape(N_SLAB, R, F)).astype(jnp.bfloat16)
        wsum = jnp.stack([sum(grads_self[1:], grads_self[0]), sum(grads_neigh[1:], grads_neigh[0])])
        return (hid, fgrad, wsum)
    hidden, feat_grad, wparts = lax.map(one_partition, jnp.arange(N_GRAPH, dtype=jnp.int32))
    w_grads = lax.optimization_barrier(jnp.sum(wparts, axis=0)) * (1.0 / jnp.sqrt(jnp.float32(ALL_ROWS)))
    return (hidden, feat_grad, smoothed_partials, smoothed_grads, w_grads)
```

```python
import functools

import jax
import jax.numpy as jnp
from jax import lax
from jax.experimental import pallas as pl
from jax.experimental.pallas import tpu as pltpu
from jax.sharding import PartitionSpec as P

SMOOTHING = 0.7
MESH = pl.DeviceIdType.MESH
XS, ZS, CORES, YS = 4, 8, 2, 4
N_GRAPH = XS * ZS * CORES
BF = jnp.bfloat16
F32 = jnp.float32


def dot(a, b):
    return lax.dot_general(a, b, (((1,), (0,)), ((), ())), preferred_element_type=F32)


def dot_tn(a, b):
    return lax.dot_general(a, b, (((0,), (0,)), ((), ())), preferred_element_type=F32)


def dot_nt(a, b):
    return lax.dot_general(a, b, (((1,), (1,)), ((), ())), preferred_element_type=F32)


def kernel(
    feats, w_self, w_neigh, vals_h, dst, src, count, pp_h, mir, cnt, mas, mom_h, cot_h, pg_h, gmom_h,
    hidden_o, fgrad_o, sp_o, sg_o, wg_o,
    group, ws, wn, vals, pp, pg, mom, cot, gmom,
    msgf, msg, inbox, a_hi, a_lo, at_hi, at_lo, own_t,
    hid_v, fg_v, sp_v, sg_v,
    wbuf, r_a, s_b, acc_a, r_b, s_c, acc_b, r_c, r_d, wfin, wg_v, s_rs, r_rs,
    lsem, osem, ag_s, ag_r, a2a_s, a2a_r, rs_s, rs_r, w_s, w_r,
):
    g = lax.axis_index("graph")
    y = lax.axis_index("slab")
    core = g % 2
    z = (g // 2) % ZS
    x = g // (2 * ZS)

    loads = {}
    for i, (name, s, d) in enumerate([
        ("pp", pp_h, pp), ("pg", pg_h, pg), ("own", feats, group.at[y]), ("vals", vals_h, vals),
        ("ws", w_self, ws), ("wn", w_neigh, wn), ("mom", mom_h, mom), ("gmom", gmom_h, gmom), ("cot", cot_h, cot),
    ]):
        loads[name] = pltpu.make_async_copy(s, d, lsem.at[i])
        loads[name].start()

    barrier = pltpu.get_barrier_semaphore()

    def sig(d, _):
        pl.semaphore_signal(barrier, inc=1, device_id=((g + d) % N_GRAPH, y), device_id_type=MESH)
        return 0

    lax.fori_loop(1, N_GRAPH, sig, 0)
    for d in range(1, YS):
        pl.semaphore_signal(barrier, inc=1, device_id=(g, (y + d) % YS), device_id_type=MESH)

    nk = 4 * N_GRAPH
    cnt_row = jnp.concatenate([cnt[...]] * 4, axis=1)
    slot_row = lax.broadcasted_iota(jnp.int32, (1, nk), 1) // N_GRAPH
    live = slot_row < cnt_row
    mir_row = jnp.concatenate([mir[c : c + 1, :] for c in range(4)], axis=1)
    mas_row = jnp.concatenate([mas[c : c + 1, :] for c in range(4)], axis=1)
    mir_row = jnp.where(live, mir_row, -1)
    rows = lax.broadcasted_iota(jnp.int32, (256, nk), 0)
    s_mir = jnp.where(rows == mir_row, 1.0, 0.0).astype(BF)
    s_mas = jnp.where(rows == mas_row, 1.0, 0.0).astype(BF)

    inbox[g] = jnp.zeros((16, 128), BF)
    for t, (name, buf, one) in enumerate([("pp", pp, s_mir), ("pg", pg, s_mas)]):
        loads[name].wait()
        out = dot_tn(one, buf[...])
        for c in range(4):
            for h in range(2):
                msgf[pl.ds(t * 8 + h * 4 + c, N_GRAPH, stride=16), :] = out[
                    c * N_GRAPH : (c + 1) * N_GRAPH, h * 128 : (h + 1) * 128
                ]
    msg[...] = msgf[...].reshape(N_GRAPH, 16, 128).astype(BF)

    pl.semaphore_wait(barrier, N_GRAPH - 1 + YS - 1)

    ag = []
    for d in range(1, YS):
        cp = pltpu.make_async_remote_copy(
            feats, group.at[y], ag_s.at[d - 1], ag_r.at[d - 1],
            device_id=(g, (y + d) % YS), device_id_type=MESH)
        cp.start()
        ag.append(cp)

    def send(d, _):
        peer = (g + d) % N_GRAPH
        pltpu.make_async_remote_copy(
            msg.at[peer], inbox.at[g], a2a_s, a2a_r, device_id=(peer, y), device_id_type=MESH).start()
        return 0

    lax.fori_loop(1, N_GRAPH, send, 0)

    loads["vals"].wait()
    n_live = count[0, 0]
    cells = []
    for b in range(32):
        cells.append(jnp.where(b < n_live, dst[0, b] * 8 + src[0, b], -1))

    def chunk(r, _):
        row = pl.multiple_of(r * 16, 16)
        acc = [jnp.zeros((16, 128), F32) for _ in range(16)]
        for b in range(32):
            v = vals[b, pl.ds(row, 16), :].astype(F32)
            for k in range(16):
                acc[k] = acc[k] + v * jnp.where(cells[b] == k, 1.0, 0.0)
        for k in range(16):
            dk, m = k // 8, k % 8
            t, col = m // 2, (m % 2) * 128
            hi = acc[k].astype(BF)
            lo = (acc[k] - hi.astype(F32)).astype(BF)
            a_hi[t, pl.ds(pl.multiple_of(dk * 128 + row, 16), 16), col : col + 128] = hi
            a_lo[t, pl.ds(pl.multiple_of(dk * 128 + row, 16), 16), col : col + 128] = lo
        return 0

    lax.fori_loop(0, 8, chunk, 0)

    for t in range(YS):
        at_hi[t] = a_hi[t].T
        at_lo[t] = a_lo[t].T
    loads["own"].wait()
    own = group[y]
    own_t[...] = own.T
    loads["ws"].wait()
    loads["wn"].wait()
    pre = dot(own, ws[...])
    local = dot(a_hi[y], own) + dot(a_lo[y], own)
    for d in range(1, YS):
        t = (y + YS - d) % YS
        ag[d - 1].wait_recv()
        tile = group[t]
        local = local + dot(a_hi[t], tile) + dot(a_lo[t], tile)

    pltpu.make_async_copy(inbox.at[pl.ds(0, N_GRAPH - 1)], inbox.at[pl.ds(0, N_GRAPH - 1)], a2a_r).wait()
    msgf[...] = inbox[...].astype(F32).reshape(N_GRAPH * 16, 128)
    got = []
    for t in range(2):
        halves = []
        for h in range(2):
            halves.append(jnp.concatenate(
                [msgf[pl.ds(t * 8 + h * 4 + c, N_GRAPH, stride=16), :] for c in range(4)], axis=0))
        got.append(jnp.concatenate(halves, axis=1).astype(BF))
    loads["mom"].wait()
    sp = SMOOTHING * mom[...] + (1.0 - SMOOTHING) * dot(s_mas, got[0])
    sp_v[...] = sp
    outs = [pltpu.make_async_copy(sp_v, sp_o, osem.at[0])]
    outs[-1].start()
    agg = (local + sp).astype(BF)
    pre = pre + dot(agg, wn[...])
    loads["cot"].wait()
    delta = jnp.where(pre > 0, cot[...], jnp.zeros((), BF))
    grads = [dot(own_t[...], delta), dot_tn(agg, delta)]
    for i in range(2):
        for h in range(2):
            wbuf[i, h * 16 : (h + 1) * 16] = grads[i][:, h * 128 : (h + 1) * 128].reshape(16, 16, 128).astype(BF)

    cp_a = pltpu.make_async_remote_copy(
        wbuf.at[1 - core], r_a, w_s.at[0], w_r.at[0], device_id=(g + 1 - 2 * core, y), device_id_type=MESH)
    cp_a.start()

    hid_v[...] = jnp.maximum(pre, 0.0).astype(BF)
    outs.append(pltpu.make_async_copy(hid_v, hidden_o, osem.at[1]))
    outs[-1].start()
    loads["gmom"].wait()
    sg = SMOOTHING * gmom[...] + (1.0 - SMOOTHING) * dot(s_mir, got[1])
    sg_v[...] = sg
    outs.append(pltpu.make_async_copy(sg_v, sg_o, osem.at[2]))
    outs[-1].start()
    gagg = (dot_nt(delta, wn[...]) + sg).astype(BF)
    rs = []
    for d in range(1, YS):
        t = (y + d) % YS
        s_rs[d - 1] = (dot(at_hi[t], gagg) + dot(at_lo[t], gagg)).astype(BF)
        cp = pltpu.make_async_remote_copy(
            s_rs.at[d - 1], r_rs.at[d - 1], rs_s.at[d - 1], rs_r.at[d - 1],
            device_id=(g, t), device_id_type=MESH)
        cp.start()
        rs.append(cp)

    for h in range(2):
        mine = jnp.where(core == 0, grads[0][:, h * 128 : (h + 1) * 128], grads[1][:, h * 128 : (h + 1) * 128])
        acc_a[h * 16 : (h + 1) * 16] = mine.reshape(16, 16, 128)
    cp_a.wait_recv()
    total = acc_a[...] + r_a[...].astype(F32)
    acc_a[...] = total
    s_b[...] = total.astype(BF)
    ops = [cp_a]

    hop = []
    for d in range(1, XS):
        px = (x + d) % XS
        cp = pltpu.make_async_remote_copy(
            s_b.at[pl.ds(px * 8, 8)], r_b.at[d - 1], w_s.at[d], w_r.at[d],
            device_id=(px * 2 * ZS + z * 2 + core, y), device_id_type=MESH)
        cp.start()
        hop.append(cp)
    fg = dot_nt(delta, ws[...]) + dot(at_hi[y], gagg) + dot(at_lo[y], gagg)
    for cp in hop:
        cp.wait_recv()
    ops += hop
    total = acc_a[pl.ds(x * 8, 8)]
    for d in range(1, XS):
        total = total + r_b[d - 1].astype(F32)
    acc_b[...] = total
    s_c[...] = total.astype(BF)

    hop = []
    for d in range(1, ZS):
        pz = (z + d) % ZS
        cp = pltpu.make_async_remote_copy(
            s_c.at[pz], r_c.at[d - 1], w_s.at[3 + d], w_r.at[3 + d],
            device_id=(x * 2 * ZS + pz * 2 + core, y), device_id_type=MESH)
        cp.start()
        hop.append(cp)
    for cp in hop:
        cp.wait_recv()
    ops += hop
    total = acc_b[z]
    for d in range(1, ZS):
        total = total + r_c[d - 1].astype(F32)
    r_d[y] = total

    hop = []
    for d in range(1, YS):
        cp = pltpu.make_async_remote_copy(
            r_d.at[y], r_d.at[y], w_s.at[10 + d], w_r.at[10 + d],
            device_id=(g, (y + d) % YS), device_id_type=MESH)
        cp.start()
        hop.append(cp)
    for cp in hop:
        cp.wait_recv()
    ops += hop
    total = ((r_d[0] + r_d[1]) + r_d[2]) + r_d[3]
    wfin[core, x * 8 + z] = total.astype(BF)

    hop = []
    for d in range(1, ZS):
        pz = (z + d) % ZS
        here = wfin.at[core, x * 8 + z]
        cp = pltpu.make_async_remote_copy(
            here, here, w_s.at[13 + d], w_r.at[13 + d],
            device_id=(x * 2 * ZS + pz * 2 + core, y), device_id_type=MESH)
        cp.start()
        hop.append(cp)
    for cp in hop:
        cp.wait_recv()
    ops += hop
    hop = []
    for d in range(1, XS):
        px = (x + d) % XS
        here = wfin.at[core, pl.ds(x * 8, 8)]
        cp = pltpu.make_async_remote_copy(
            here, here, w_s.at[20 + d], w_r.at[20 + d],
            device_id=(px * 2 * ZS + z * 2 + core, y), device_id_type=MESH)
        cp.start()
        hop.append(cp)
    for cp in hop:
        cp.wait_recv()
    ops += hop
    here = wfin.at[core]
    last = pltpu.make_async_remote_copy(
        here, here, w_s.at[24], w_r.at[24], device_id=(g + 1 - 2 * core, y), device_id_type=MESH)
    last.start()
    ops.append(last)

    for cp in rs:
        cp.wait_recv()
    for d in range(1, YS):
        fg = fg + r_rs[d - 1].astype(F32)
    fg_v[...] = fg.astype(BF)
    outs.append(pltpu.make_async_copy(fg_v, fgrad_o, osem.at[3]))
    outs[-1].start()

    last.wait_recv()
    scale = 1.0 / (N_GRAPH * YS * 256) ** 0.5
    for i in range(2):
        for h in range(2):
            wg_v[i, :, h * 128 : (h + 1) * 128] = (
                wfin[i, h * 16 : (h + 1) * 16].astype(F32).reshape(256, 128) * scale)
    outs.append(pltpu.make_async_copy(wg_v, wg_o, osem.at[4]))
    outs[-1].start()

    for cp in ag + rs + ops:
        cp.wait_send()
    pltpu.make_async_copy(msg.at[pl.ds(0, N_GRAPH - 1)], msg.at[pl.ds(0, N_GRAPH - 1)], a2a_s).wait()
    for cp in outs:
        cp.wait()


def shards(
    feats, w_self, w_neigh, block_vals, block_dst, block_src, block_count, prev_partial,
    mirror_rows, send_count, master_rows, momentum, cotangent, prev_grad, grad_momentum,
):
    sds = jax.ShapeDtypeStruct
    hbm = pl.BlockSpec(memory_space=pl.ANY)
    vm = pl.BlockSpec(memory_space=pltpu.VMEM)
    sm = pl.BlockSpec(memory_space=pltpu.SMEM)
    V = pltpu.VMEM
    dma = pltpu.SemaphoreType.DMA
    mat = lambda dt: V((256, 256), dt)
    hidden, fgrad, sp, sg, wg = pl.pallas_call(
        kernel,
        out_shape=(
            sds((256, 256), BF), sds((256, 256), BF), sds((256, 256), F32), sds((256, 256), F32),
            sds((2, 256, 256), F32),
        ),
        in_specs=[hbm, hbm, hbm, hbm, sm, sm, sm, hbm, vm, vm, vm, hbm, hbm, hbm, hbm],
        out_specs=[hbm] * 5,
        scratch_shapes=[
            V((YS, 256, 256), BF), mat(BF), mat(BF), V((32, 128, 128), BF), mat(BF), mat(BF), mat(F32), mat(BF), mat(F32),
            V((N_GRAPH * 16, 128), F32), V((N_GRAPH, 16, 128), BF), V((N_GRAPH, 16, 128), BF),
            V((YS, 256, 256), BF), V((YS, 256, 256), BF), V((YS, 256, 256), BF), V((YS, 256, 256), BF), mat(BF),
            mat(BF), mat(BF), mat(F32), mat(F32),
            V((2, 32, 16, 128), BF), V((32, 16, 128), BF), V((32, 16, 128), BF), V((32, 16, 128), F32),
            V((XS - 1, 8, 16, 128), BF), V((8, 16, 128), BF), V((8, 16, 128), F32), V((ZS - 1, 16, 128), BF),
            V((YS, 16, 128), F32), V((2, 32, 16, 128), BF), V((2, 256, 256), F32),
            V((YS - 1, 256, 256), BF), V((YS - 1, 256, 256), BF),
            dma((9,)), dma((5,)), dma((YS - 1,)), dma((YS - 1,)), dma, dma, dma((YS - 1,)), dma((YS - 1,)),
            dma((25,)), dma((25,)),
        ],
        compiler_params=pltpu.CompilerParams(
            collective_id=0, has_side_effects=True, vmem_limit_bytes=62 * 1024 * 1024),
    )(
        feats[0, 0], w_self, w_neigh, block_vals[0, 0], block_dst[0], block_src[0], block_count,
        prev_partial[0, 0], jnp.swapaxes(mirror_rows[0, 0], 0, 1), send_count[0], jnp.swapaxes(master_rows[0, 0], 0, 1),
        momentum[0, 0], cotangent[0, 0], prev_grad[0, 0], grad_momentum[0, 0],
    )
    return hidden[None, None], fgrad[None, None], sp[None, None], sg[None, None], wg


def solution(mesh):
    gs = lambda n: P("graph", "slab", *([None] * n))
    in_specs = (
        gs(2), P(), P(), gs(3), gs(1), gs(1), gs(0), gs(2), gs(2), gs(1), gs(2), gs(2), gs(2), gs(2), gs(2),
    )
    out_specs = (gs(2), gs(2), gs(2), gs(2), P())
    return jax.shard_map(shards, mesh=mesh, in_specs=in_specs, out_specs=out_specs, check_vma=False)
```

```python
import functools

import jax
import jax.numpy as jnp
from jax import lax
from jax.experimental import pallas as pl
from jax.experimental.pallas import tpu as pltpu
from jax.sharding import PartitionSpec as P

SMOOTHING = 0.7
MESH = pl.DeviceIdType.MESH
XS, ZS, CORES, YS = 4, 8, 2, 4
N_GRAPH = XS * ZS * CORES
CHIPS = XS * ZS
BF = jnp.bfloat16
F32 = jnp.float32


def dot(a, b):
    return lax.dot_general(a, b, (((1,), (0,)), ((), ())), preferred_element_type=F32)


def dot_tn(a, b):
    return lax.dot_general(a, b, (((0,), (0,)), ((), ())), preferred_element_type=F32)


def dot_nt(a, b):
    return lax.dot_general(a, b, (((1,), (1,)), ((), ())), preferred_element_type=F32)


def kernel(
    feats, w_self, w_neigh, vals_h, dst, src, count, pp_h, mir, cnt, mas, mom_h, cot_h, pg_h, gmom_h,
    hidden_o, fgrad_o, sp_o, sg_o, wg_o,
    group, ws, wn, vals, pp, pg, mom, cot, gmom,
    msgf, msg, inbox, a_hi, a_lo, at_hi, at_lo,
    hid_v, fg_v, sp_v, sg_v,
    s_a, r_a, s_b, acc_a, r_b, r_c, wfin, wg_v, s_rs, r_rs,
    lsem, osem, ag_s, ag_r, a2a_s, a2a_r, fw_s, fw_r, rs_s, rs_r, w_s, w_r,
):
    g = lax.axis_index("graph")
    y = lax.axis_index("slab")
    core = g % 2
    chip = g // 2
    z = chip % ZS
    x = chip // ZS
    sibling = (g + 1 - 2 * core, y)
    plane = [(dx, dy) for dx in range(XS) for dy in range(YS) if dx or dy]

    def at_plane(dx, dy):
        return ((x + dx) % XS, (y + dy) % YS)

    def device(px, pz, py):
        return ((px * ZS + pz) * 2 + core, py)

    loads = {}
    for i, (name, s, d) in enumerate([
        ("pp", pp_h, pp), ("pg", pg_h, pg), ("own", feats, group.at[y]), ("vals", vals_h, vals),
        ("ws", w_self, ws), ("wn", w_neigh, wn), ("mom", mom_h, mom), ("gmom", gmom_h, gmom), ("cot", cot_h, cot),
    ]):
        loads[name] = pltpu.make_async_copy(s, d, lsem.at[i])
        loads[name].start()

    barrier = pltpu.get_barrier_semaphore()

    def greet(peer):
        pl.semaphore_signal(barrier, inc=1, device_id=peer, device_id_type=MESH)

    def sig(d, _):
        greet((((chip + d) % CHIPS) * 2 + core, y))
        return 0

    lax.fori_loop(1, CHIPS, sig, 0)
    greet(sibling)
    away = [(dx, dy) for dx, dy in plane if dy]
    for dx, dy in away:
        px, py = at_plane(dx, dy)
        greet(device(px, z, py))

    nk = 4 * N_GRAPH
    cnt_row = jnp.concatenate([cnt[...]] * 4, axis=1)
    slot_row = lax.broadcasted_iota(jnp.int32, (1, nk), 1) // N_GRAPH
    live = slot_row < cnt_row
    mir_row = jnp.concatenate([mir[c : c + 1, :] for c in range(4)], axis=1)
    mas_row = jnp.concatenate([mas[c : c + 1, :] for c in range(4)], axis=1)
    mir_row = jnp.where(live, mir_row, -1)
    rows = lax.broadcasted_iota(jnp.int32, (256, nk), 0)
    s_mir = jnp.where(rows == mir_row, 1.0, 0.0).astype(BF)
    s_mas = jnp.where(rows == mas_row, 1.0, 0.0).astype(BF)

    for t, (name, buf, one) in enumerate([("pp", pp, s_mir), ("pg", pg, s_mas)]):
        loads[name].wait()
        out = dot_tn(one, buf[...])
        for c in range(4):
            for h in range(2):
                msgf[t, pl.ds(h * 4 + c, N_GRAPH, stride=8), :] = out[
                    c * N_GRAPH : (c + 1) * N_GRAPH, h * 128 : (h + 1) * 128
                ]
        msg[t] = msgf[t].reshape(CHIPS, 16, 128).astype(BF)
        inbox[t, chip, core] = msg[t, chip]

    pl.semaphore_wait(barrier, CHIPS + len(away))

    ag = []
    for d in range(1, YS):
        cp = pltpu.make_async_remote_copy(
            feats, group.at[y], ag_s.at[d - 1], ag_r.at[d - 1],
            device_id=(g, (y + d) % YS), device_id_type=MESH)
        cp.start()
        ag.append(cp)

    for t in range(2):

        def send(d, _):
            peer = (chip + d) % CHIPS
            pltpu.make_async_remote_copy(
                msg.at[t, peer], inbox.at[t, chip, core], a2a_s.at[t], a2a_r.at[t],
                device_id=(peer * 2 + core, y), device_id_type=MESH).start()
            return 0

        lax.fori_loop(1, CHIPS, send, 0)

    def forward(t):
        some = inbox.at[t, pl.ds(0, CHIPS - 1), 0]
        pltpu.make_async_copy(some, some, a2a_r.at[t]).wait()
        cp = pltpu.make_async_remote_copy(
            inbox.at[t, :, core], inbox.at[t, :, core], fw_s.at[t], fw_r.at[t],
            device_id=sibling, device_id_type=MESH)
        cp.start()
        return cp

    def received(t):
        both = inbox[t].astype(F32).reshape(N_GRAPH, 16, 128)
        msgf[t] = jnp.where(core == 0, both[:, :8], both[:, 8:]).reshape(N_GRAPH * 8, 128)
        halves = []
        for h in range(2):
            halves.append(jnp.concatenate(
                [msgf[t, pl.ds(h * 4 + c, N_GRAPH, stride=8), :] for c in range(4)], axis=0))
        return jnp.concatenate(halves, axis=1).astype(BF)

    loads["vals"].wait()
    n_live = count[0, 0]
    cells = []
    for b in range(32):
        cells.append(jnp.where(b < n_live, dst[0, b] * 8 + src[0, b], -1))

    def chunk(r, _):
        row = pl.multiple_of(r * 16, 16)
        acc = [jnp.zeros((16, 128), F32) for _ in range(16)]
        for b in range(32):
            v = vals[b, pl.ds(row, 16), :].astype(F32)
            for k in range(16):
                acc[k] = acc[k] + v * jnp.where(cells[b] == k, 1.0, 0.0)
        for k in range(16):
            dk, m = k // 8, k % 8
            t, col = m // 2, (m % 2) * 128
            hi = acc[k].astype(BF)
            lo = (acc[k] - hi.astype(F32)).astype(BF)
            a_hi[t, pl.ds(pl.multiple_of(dk * 128 + row, 16), 16), col : col + 128] = hi
            a_lo[t, pl.ds(pl.multiple_of(dk * 128 + row, 16), 16), col : col + 128] = lo
        return 0

    lax.fori_loop(0, 8, chunk, 0)

    for t in range(YS):
        at_hi[t] = a_hi[t].T
        at_lo[t] = a_lo[t].T
    loads["own"].wait()
    own = group[y]
    loads["ws"].wait()
    loads["wn"].wait()
    pre = dot(own, ws[...])
    local = dot(a_hi[y], own) + dot(a_lo[y], own)
    for d in range(1, YS):
        t = (y + YS - d) % YS
        ag[d - 1].wait_recv()
        tile = group[t]
        local = local + dot(a_hi[t], tile) + dot(a_lo[t], tile)

    fw = [forward(0)]
    loads["mom"].wait()
    loads["cot"].wait()
    fw[0].wait_recv()
    sp = SMOOTHING * mom[...] + (1.0 - SMOOTHING) * dot(s_mas, received(0))
    agg = (local + sp).astype(BF)
    pre = pre + dot(agg, wn[...])
    delta = jnp.where(pre > 0, cot[...], jnp.zeros((), BF))

    def tiles(m, h):
        return m[:, h * 128 : (h + 1) * 128].reshape(16, 16, 128)

    given = dot_tn(jnp.where(core == 0, agg, own), delta)
    for h in range(2):
        s_a[h * 16 : (h + 1) * 16] = tiles(given, h).astype(BF)
    cp_a = pltpu.make_async_remote_copy(
        s_a, r_a, w_s.at[0], w_r.at[0], device_id=sibling, device_id_type=MESH)
    cp_a.start()
    fw.append(forward(1))
    kept = dot_tn(jnp.where(core == 0, own, agg), delta)
    cp_a.wait_recv()
    for h in range(2):
        part = slice(h * 16, (h + 1) * 16)
        total = tiles(kept, h) + r_a[part].astype(F32)
        acc_a[part] = total
        s_b[part] = total.astype(BF)
    ops = [cp_a]

    place = x * YS + y
    hop = []
    for i, (dx, dy) in enumerate(plane):
        px, py = at_plane(dx, dy)
        cp = pltpu.make_async_remote_copy(
            s_b.at[pl.ds((px * YS + py) * 2, 2)], r_b.at[i], w_s.at[1 + i], w_r.at[1 + i],
            device_id=device(px, z, py), device_id_type=MESH)
        cp.start()
        hop.append(cp)

    sp_v[...] = sp
    outs = [pltpu.make_async_copy(sp_v, sp_o, osem.at[0])]
    outs[-1].start()
    hid_v[...] = jnp.maximum(pre, 0.0).astype(BF)
    outs.append(pltpu.make_async_copy(hid_v, hidden_o, osem.at[1]))
    outs[-1].start()
    loads["gmom"].wait()
    fw[1].wait_recv()
    sg = SMOOTHING * gmom[...] + (1.0 - SMOOTHING) * dot(s_mir, received(1))
    sg_v[...] = sg
    outs.append(pltpu.make_async_copy(sg_v, sg_o, osem.at[2]))
    outs[-1].start()
    gagg = (dot_nt(delta, wn[...]) + sg).astype(BF)
    rs = []
    for d in range(1, YS):
        t = (y + d) % YS
        s_rs[d - 1] = (dot(at_hi[t], gagg) + dot(at_lo[t], gagg)).astype(BF)
        cp = pltpu.make_async_remote_copy(
            s_rs.at[d - 1], r_rs.at[d - 1], rs_s.at[d - 1], rs_r.at[d - 1],
            device_id=(g, t), device_id_type=MESH)
        cp.start()
        rs.append(cp)

    for cp in hop:
        cp.wait_recv()
    ops += hop
    total = acc_a[pl.ds(place * 2, 2)]
    for i in range(len(plane)):
        total = total + r_b[i].astype(F32)

    r_c[z] = total.astype(BF)
    hop = []
    for d in range(1, ZS):
        cp = pltpu.make_async_remote_copy(
            r_c.at[z], r_c.at[z], w_s.at[15 + d], w_r.at[15 + d],
            device_id=device(x, (z + d) % ZS, y), device_id_type=MESH)
        cp.start()
        hop.append(cp)
    fg = dot_nt(delta, ws[...]) + dot(at_hi[y], gagg) + dot(at_lo[y], gagg)
    for cp in hop:
        cp.wait_recv()
    ops += hop
    total = r_c[0].astype(F32)
    for i in range(1, ZS):
        total = total + r_c[i].astype(F32)
    mine = wfin.at[core, pl.ds(place * 2, 2)]
    mine[...] = total.astype(BF)

    hop = []
    for i, (dx, dy) in enumerate(plane):
        px, py = at_plane(dx, dy)
        cp = pltpu.make_async_remote_copy(
            mine, mine, w_s.at[23 + i], w_r.at[23 + i], device_id=device(px, z, py), device_id_type=MESH)
        cp.start()
        hop.append(cp)
    for cp in rs:
        cp.wait_recv()
    for d in range(1, YS):
        fg = fg + r_rs[d - 1].astype(F32)
    fg_v[...] = fg.astype(BF)
    outs.append(pltpu.make_async_copy(fg_v, fgrad_o, osem.at[3]))
    outs[-1].start()

    for cp in hop:
        cp.wait_recv()
    ops += hop
    last = pltpu.make_async_remote_copy(
        wfin.at[core], wfin.at[core], w_s.at[38], w_r.at[38], device_id=sibling, device_id_type=MESH)
    last.start()
    ops.append(last)
    last.wait_recv()
    scale = 1.0 / (N_GRAPH * YS * 256) ** 0.5
    for i in range(2):
        for h in range(2):
            wg_v[i, :, h * 128 : (h + 1) * 128] = (
                wfin[i, h * 16 : (h + 1) * 16].astype(F32).reshape(256, 128) * scale)
    outs.append(pltpu.make_async_copy(wg_v, wg_o, osem.at[4]))
    outs[-1].start()

    for cp in ag + fw + rs + ops:
        cp.wait_send()
    for t in range(2):
        some = msg.at[t, pl.ds(0, CHIPS - 1)]
        pltpu.make_async_copy(some, some, a2a_s.at[t]).wait()
    for cp in outs:
        cp.wait()


def hand_over(*refs):
    results, outs, stage, sem = refs[:5], refs[5:10], refs[10:15], refs[15]
    order = (4, 2, 3, 0, 1)
    pull = [pltpu.make_async_copy(results[i], stage[i], sem.at[i]) for i in range(5)]
    push = [pltpu.make_async_copy(stage[i], outs[i], sem.at[5 + i]) for i in range(5)]
    for i in order:
        pull[i].start()
    for i in order:
        pull[i].wait()
        push[i].start()
    for i in order:
        push[i].wait()


def shards(
    feats, w_self, w_neigh, block_vals, block_dst, block_src, block_count, prev_partial,
    mirror_rows, send_count, master_rows, momentum, cotangent, prev_grad, grad_momentum,
):
    sds = jax.ShapeDtypeStruct
    hbm = pl.BlockSpec(memory_space=pl.ANY)
    vm = pl.BlockSpec(memory_space=pltpu.VMEM)
    sm = pl.BlockSpec(memory_space=pltpu.SMEM)
    V = pltpu.VMEM
    dma = pltpu.SemaphoreType.DMA
    mat = lambda dt: V((256, 256), dt)
    results = pl.pallas_call(
        kernel,
        out_shape=(
            sds((256, 256), BF), sds((256, 256), BF), sds((256, 256), F32), sds((256, 256), F32),
            sds((2, 256, 256), F32),
        ),
        in_specs=[hbm, hbm, hbm, hbm, sm, sm, sm, hbm, vm, vm, vm, hbm, hbm, hbm, hbm],
        out_specs=[hbm] * 5,
        scratch_shapes=[
            V((YS, 256, 256), BF), mat(BF), mat(BF), V((32, 128, 128), BF), mat(BF), mat(BF), mat(F32), mat(BF), mat(F32),
            V((2, N_GRAPH * 8, 128), F32), V((2, CHIPS, 16, 128), BF), V((2, CHIPS, CORES, 16, 128), BF),
            V((YS, 256, 256), BF), V((YS, 256, 256), BF), V((YS, 256, 256), BF), V((YS, 256, 256), BF),
            mat(BF), mat(BF), mat(F32), mat(F32),
            V((32, 16, 128), BF), V((32, 16, 128), BF), V((32, 16, 128), BF), V((32, 16, 128), F32),
            V((XS * YS - 1, 2, 16, 128), BF), V((ZS, 2, 16, 128), BF), V((2, 32, 16, 128), BF), V((2, 256, 256), F32),
            V((YS - 1, 256, 256), BF), V((YS - 1, 256, 256), BF),
            dma((9,)), dma((5,)), dma((YS - 1,)), dma((YS - 1,)), dma((2,)), dma((2,)), dma((2,)), dma((2,)),
            dma((YS - 1,)), dma((YS - 1,)), dma((39,)), dma((39,)),
        ],
        compiler_params=pltpu.CompilerParams(
            collective_id=0, has_side_effects=True, vmem_limit_bytes=62 * 1024 * 1024),
    )(
        feats[0, 0], w_self, w_neigh, block_vals[0, 0], block_dst[0], block_src[0], block_count,
        prev_partial[0, 0], jnp.swapaxes(mirror_rows[0, 0], 0, 1), send_count[0], jnp.swapaxes(master_rows[0, 0], 0, 1),
        momentum[0, 0], cotangent[0, 0], prev_grad[0, 0], grad_momentum[0, 0],
    )
    hidden, fgrad, sp, sg, wg = pl.pallas_call(
        hand_over,
        out_shape=tuple(sds(r.shape, r.dtype) for r in results),
        in_specs=[hbm] * 5,
        out_specs=[hbm] * 5,
        scratch_shapes=[V(r.shape, r.dtype) for r in results] + [dma((10,))],
        compiler_params=pltpu.CompilerParams(vmem_limit_bytes=62 * 1024 * 1024),
    )(*results)
    return hidden[None, None], fgrad[None, None], sp[None, None], sg[None, None], wg


def solution(mesh):
    gs = lambda n: P("graph", "slab", *([None] * n))
    in_specs = (
        gs(2), P(), P(), gs(3), gs(1), gs(1), gs(0), gs(2), gs(2), gs(1), gs(2), gs(2), gs(2), gs(2), gs(2),
    )
    out_specs = (gs(2), gs(2), gs(2), gs(2), P())
    return jax.shard_map(shards, mesh=mesh, in_specs=in_specs, out_specs=out_specs, check_vma=False)
```

```python
import functools

import jax
import jax.numpy as jnp
from jax import lax
from jax.experimental import pallas as pl
from jax.experimental.pallas import tpu as pltpu
from jax.sharding import PartitionSpec as P

SMOOTHING = 0.7
MESH = pl.DeviceIdType.MESH
XS, ZS, CORES, YS = 4, 8, 2, 4
N_GRAPH = XS * ZS * CORES
CHIPS = XS * ZS
BF = jnp.bfloat16
F32 = jnp.float32
I32 = jnp.int32


def dot(a, b):
    return lax.dot_general(a, b, (((1,), (0,)), ((), ())), preferred_element_type=F32)


def dot_tn(a, b):
    return lax.dot_general(a, b, (((0,), (0,)), ((), ())), preferred_element_type=F32)


def dot_nt(a, b):
    return lax.dot_general(a, b, (((1,), (1,)), ((), ())), preferred_element_type=F32)


def kernel(
    feats, w_self, w_neigh, vals_h, dst_h, src_h, count_h, pp_h, mir_h, cnt_h, mas_h, mom_h, cot_h, pg_h, gmom_h,
    hidden_o, fgrad_o, sp_o, sg_o, wg_o,
    group, ws, wn, vals, pp, pg, mom, cot, gmom, mir, mas, cnt, dst, src, count,
    msgf, msg, inbox, a_hi, a_lo, at_hi, at_lo,
    hid_v, fg_v, sp_v, sg_v,
    s_a, r_a, s_b, acc_a, r_b, r_c, wfin, s_rs, r_rs,
    lsem, osem, ag_s, ag_r, a2a_s, a2a_r, fw_s, fw_r, rs_s, rs_r, w_s, w_r,
):
    g = lax.axis_index("graph")
    y = lax.axis_index("slab")
    core = g % 2
    chip = g // 2
    z = chip % ZS
    x = chip // ZS
    sibling = (g + 1 - 2 * core, y)
    def near(d, n):
        return min(d, n - d)

    plane = [(dx, dy) for dx in range(XS) for dy in range(YS) if dx or dy]
    plane.sort(key=lambda o: -near(o[0], XS) - near(o[1], YS))
    sheet = [(dx, dz) for dx in range(XS) for dz in range(ZS) if dx or dz]
    sheet.sort(key=lambda o: -near(o[0], XS) - near(o[1], ZS))
    line = sorted(range(1, ZS), key=lambda d: -near(d, ZS))
    slabs = sorted(range(1, YS), key=lambda d: -near(d, YS))


    def at_plane(dx, dy):
        return ((x + dx) % XS, (y + dy) % YS)

    def device(px, pz, py):
        return ((px * ZS + pz) * 2 + core, py)

    barrier = pltpu.get_barrier_semaphore()

    def greet(peer):
        pl.semaphore_signal(barrier, inc=1, device_id=peer, device_id_type=MESH)

    for dx, dz in sheet:
        greet(device((x + dx) % XS, (z + dz) % ZS, y))
    greet(sibling)
    away = [(dx, dy) for dx, dy in plane if dy]
    for dx, dy in away:
        px, py = at_plane(dx, dy)
        greet(device(px, z, py))

    loads = {}
    for i, (name, s, d) in enumerate([
        ("mir", mir_h, mir), ("cnt", cnt_h, cnt), ("pp", pp_h, pp), ("mas", mas_h, mas), ("pg", pg_h, pg), ("own", feats, group.at[y]), ("vals", vals_h, vals),
        ("ws", w_self, ws), ("wn", w_neigh, wn), ("mom", mom_h, mom), ("gmom", gmom_h, gmom), ("cot", cot_h, cot),
        ("dst", dst_h, dst), ("src", src_h, src), ("count", count_h, count),
    ]):
        loads[name] = pltpu.make_async_copy(s, d, lsem.at[i])
        loads[name].start()

    for name in ("mir", "cnt", "mas"):
        loads[name].wait()
    nk = 4 * N_GRAPH
    cnt_row = jnp.concatenate([cnt[...]] * 4, axis=1)
    slot_row = lax.broadcasted_iota(jnp.int32, (1, nk), 1) // N_GRAPH
    live = slot_row < cnt_row
    mir_row = jnp.concatenate([mir[c : c + 1, :] for c in range(4)], axis=1)
    mas_row = jnp.concatenate([mas[c : c + 1, :] for c in range(4)], axis=1)
    mir_row = jnp.where(live, mir_row, -1)
    rows = lax.broadcasted_iota(jnp.int32, (256, nk), 0)
    s_mir = jnp.where(rows == mir_row, 1.0, 0.0).astype(BF)
    s_mas = jnp.where(rows == mas_row, 1.0, 0.0).astype(BF)

    for t, (name, buf, one) in enumerate([("pp", pp, s_mir), ("pg", pg, s_mas)]):
        loads[name].wait()
        out = dot_tn(one, buf[...])
        for c in range(4):
            for h in range(2):
                msgf[t, pl.ds(h * 4 + c, N_GRAPH, stride=8), :] = out[
                    c * N_GRAPH : (c + 1) * N_GRAPH, h * 128 : (h + 1) * 128
                ]
        msg[t] = msgf[t].reshape(CHIPS, 16, 128).astype(BF)
        inbox[t, chip, core] = msg[t, chip]

    pl.semaphore_wait(barrier, CHIPS + len(away))

    ag = {}
    for d in slabs:
        cp = pltpu.make_async_remote_copy(
            feats, group.at[y], ag_s.at[d - 1], ag_r.at[d - 1],
            device_id=(g, (y + d) % YS), device_id_type=MESH)
        cp.start()
        ag[d] = cp

    for t in range(2):
        for dx, dz in sheet:
            px, pz = (x + dx) % XS, (z + dz) % ZS
            pltpu.make_async_remote_copy(
                msg.at[t, px * ZS + pz], inbox.at[t, chip, core], a2a_s.at[t], a2a_r.at[t],
                device_id=device(px, pz, y), device_id_type=MESH).start()

    def forward(t):
        some = inbox.at[t, pl.ds(0, CHIPS - 1), 0]
        pltpu.make_async_copy(some, some, a2a_r.at[t]).wait()
        cp = pltpu.make_async_remote_copy(
            inbox.at[t, :, core], inbox.at[t, :, core], fw_s.at[t], fw_r.at[t],
            device_id=sibling, device_id_type=MESH)
        cp.start()
        return cp

    def received(t):
        both = inbox[t].astype(F32).reshape(N_GRAPH, 16, 128)
        msgf[t] = jnp.where(core == 0, both[:, :8], both[:, 8:]).reshape(N_GRAPH * 8, 128)
        halves = []
        for h in range(2):
            halves.append(jnp.concatenate(
                [msgf[t, pl.ds(h * 4 + c, N_GRAPH, stride=8), :] for c in range(4)], axis=0))
        return jnp.concatenate(halves, axis=1).astype(BF)

    loads["vals"].wait()
    for name in ("dst", "src", "count"):
        loads[name].wait()
    n_live = count[0, 0]
    cells = []
    for b in range(32):
        cells.append(jnp.where(b < n_live, dst[0, b] * 8 + src[0, b], -1))

    def chunk(r, _):
        row = pl.multiple_of(r * 16, 16)
        acc = [jnp.zeros((16, 128), F32) for _ in range(16)]
        for b in range(32):
            v = vals[b, pl.ds(row, 16), :].astype(F32)
            for k in range(16):
                acc[k] = acc[k] + v * jnp.where(cells[b] == k, 1.0, 0.0)
        for k in range(16):
            dk, m = k // 8, k % 8
            t, col = m // 2, (m % 2) * 128
            hi = acc[k].astype(BF)
            lo = (acc[k] - hi.astype(F32)).astype(BF)
            a_hi[t, pl.ds(pl.multiple_of(dk * 128 + row, 16), 16), col : col + 128] = hi
            a_lo[t, pl.ds(pl.multiple_of(dk * 128 + row, 16), 16), col : col + 128] = lo
        return 0

    lax.fori_loop(0, 8, chunk, 0)

    for t in range(YS):
        at_hi[t] = a_hi[t].T
        at_lo[t] = a_lo[t].T
    loads["own"].wait()
    own = group[y]
    loads["ws"].wait()
    loads["wn"].wait()
    pre = dot(own, ws[...])
    local = dot(a_hi[y], own) + dot(a_lo[y], own)
    for d in slabs[::-1]:
        t = (y + YS - d) % YS
        ag[d].wait_recv()
        tile = group[t]
        local = local + dot(a_hi[t], tile) + dot(a_lo[t], tile)

    fw = [forward(0)]
    loads["mom"].wait()
    loads["cot"].wait()
    fw[0].wait_recv()
    sp = SMOOTHING * mom[...] + (1.0 - SMOOTHING) * dot(s_mas, received(0))
    agg = (local + sp).astype(BF)
    pre = pre + dot(agg, wn[...])
    delta = jnp.where(pre > 0, cot[...], jnp.zeros((), BF))

    def tiles(m, h):
        return m[:, h * 128 : (h + 1) * 128].reshape(16, 16, 128)

    given = dot_tn(jnp.where(core == 0, agg, own), delta)
    for h in range(2):
        s_a[h * 16 : (h + 1) * 16] = tiles(given, h).astype(BF)
    cp_a = pltpu.make_async_remote_copy(
        s_a, r_a, w_s.at[0], w_r.at[0], device_id=sibling, device_id_type=MESH)
    cp_a.start()
    fw.append(forward(1))
    kept = dot_tn(jnp.where(core == 0, own, agg), delta)
    cp_a.wait_recv()
    for h in range(2):
        part = slice(h * 16, (h + 1) * 16)
        total = tiles(kept, h) + r_a[part].astype(F32)
        acc_a[part] = total
        s_b[part] = total.astype(BF)
    ops = [cp_a]

    place = x * YS + y
    hop = []
    for i, (dx, dy) in enumerate(plane):
        px, py = at_plane(dx, dy)
        cp = pltpu.make_async_remote_copy(
            s_b.at[pl.ds((px * YS + py) * 2, 2)], r_b.at[i], w_s.at[1 + i], w_r.at[1 + i],
            device_id=device(px, z, py), device_id_type=MESH)
        cp.start()
        hop.append(cp)

    sp_v[...] = sp
    outs = [pltpu.make_async_copy(sp_v, sp_o, osem.at[0])]
    outs[-1].start()
    hid_v[...] = jnp.maximum(pre, 0.0).astype(BF)
    outs.append(pltpu.make_async_copy(hid_v, hidden_o, osem.at[1]))
    outs[-1].start()
    loads["gmom"].wait()
    fw[1].wait_recv()
    sg = SMOOTHING * gmom[...] + (1.0 - SMOOTHING) * dot(s_mir, received(1))
    sg_v[...] = sg
    outs.append(pltpu.make_async_copy(sg_v, sg_o, osem.at[2]))
    outs[-1].start()
    gagg = (dot_nt(delta, wn[...]) + sg).astype(BF)
    rs = []
    for d in slabs:
        t = (y + d) % YS
        s_rs[d - 1] = (dot(at_hi[t], gagg) + dot(at_lo[t], gagg)).astype(BF)
        cp = pltpu.make_async_remote_copy(
            s_rs.at[d - 1], r_rs.at[d - 1], rs_s.at[d - 1], rs_r.at[d - 1],
            device_id=(g, t), device_id_type=MESH)
        cp.start()
        rs.append(cp)

    for cp in hop:
        cp.wait_recv()
    ops += hop
    total = acc_a[pl.ds(place * 2, 2)]
    for i in range(len(plane)):
        total = total + r_b[i].astype(F32)

    r_c[z] = total.astype(BF)
    hop = []
    for d in line:
        cp = pltpu.make_async_remote_copy(
            r_c.at[z], r_c.at[z], w_s.at[15 + d], w_r.at[15 + d],
            device_id=device(x, (z + d) % ZS, y), device_id_type=MESH)
        cp.start()
        hop.append(cp)
    fg = dot_nt(delta, ws[...]) + dot(at_hi[y], gagg) + dot(at_lo[y], gagg)
    for cp in hop:
        cp.wait_recv()
    ops += hop
    total = r_c[0].astype(F32)
    for i in range(1, ZS):
        total = total + r_c[i].astype(F32)
    mine = wfin.at[core, pl.ds(place * 2, 2)]
    mine[...] = total.astype(BF)

    hop = []
    for i, (dx, dy) in enumerate(plane):
        px, py = at_plane(dx, dy)
        cp = pltpu.make_async_remote_copy(
            mine, mine, w_s.at[23 + i], w_r.at[23 + i], device_id=device(px, z, py), device_id_type=MESH)
        cp.start()
        hop.append(cp)
    for cp in rs:
        cp.wait_recv()
    for d in range(1, YS):
        fg = fg + r_rs[d - 1].astype(F32)
    fg_v[...] = fg.astype(BF)
    outs.append(pltpu.make_async_copy(fg_v, fgrad_o, osem.at[3]))
    outs[-1].start()

    for cp in hop:
        cp.wait_recv()
    ops += hop
    last = pltpu.make_async_remote_copy(
        wfin.at[core], wg_o.at[core], w_s.at[38], w_r.at[38], device_id=sibling, device_id_type=MESH)
    last.start()
    ops.append(last)
    outs.append(pltpu.make_async_copy(wfin.at[core], wg_o.at[core], osem.at[4]))
    outs[-1].start()
    last.wait_recv()

    for cp in list(ag.values()) + fw + rs + ops:
        cp.wait_send()
    for t in range(2):
        some = msg.at[t, pl.ds(0, CHIPS - 1)]
        pltpu.make_async_copy(some, some, a2a_s.at[t]).wait()
    for cp in outs:
        cp.wait()


def hand_over(*refs):
    results, outs, stage, wide, sem = refs[:5], refs[5:10], refs[10:15], refs[15], refs[16]
    order = (4, 2, 3, 0, 1)
    pull = [pltpu.make_async_copy(results[i], stage[i], sem.at[i]) for i in range(5)]
    push = [pltpu.make_async_copy(wide if i == 4 else stage[i], outs[i], sem.at[5 + i]) for i in range(5)]
    for i in order:
        pull[i].start()
    for i in order:
        pull[i].wait()
        if i == 4:
            scale = 1.0 / (N_GRAPH * YS * 256) ** 0.5
            for k in range(2):
                for h in range(2):
                    wide[k, :, h * 128 : (h + 1) * 128] = (
                        stage[4][k, h * 16 : (h + 1) * 16].astype(F32).reshape(256, 128) * scale)
        push[i].start()
    for i in order:
        push[i].wait()


def shards(
    feats, w_self, w_neigh, block_vals, block_dst, block_src, block_count, prev_partial,
    mirror_rows, send_count, master_rows, momentum, cotangent, prev_grad, grad_momentum,
):
    sds = jax.ShapeDtypeStruct
    hbm = pl.BlockSpec(memory_space=pl.ANY)
    V, S = pltpu.VMEM, pltpu.SMEM
    dma = pltpu.SemaphoreType.DMA
    mat = lambda dt: V((256, 256), dt)
    results = pl.pallas_call(
        kernel,
        out_shape=(
            sds((256, 256), BF), sds((256, 256), BF), sds((256, 256), F32), sds((256, 256), F32),
            sds((2, 32, 16, 128), BF),
        ),
        in_specs=[hbm] * 15,
        out_specs=[hbm] * 5,
        scratch_shapes=[
            V((YS, 256, 256), BF), mat(BF), mat(BF), V((32, 128, 128), BF), mat(BF), mat(BF), mat(F32), mat(BF), mat(F32),
            V((4, N_GRAPH), I32), V((4, N_GRAPH), I32), V((1, N_GRAPH), I32), S((1, 32), I32), S((1, 32), I32), S((1, 1), I32),
            V((2, N_GRAPH * 8, 128), F32), V((2, CHIPS, 16, 128), BF), V((2, CHIPS, CORES, 16, 128), BF),
            V((YS, 256, 256), BF), V((YS, 256, 256), BF), V((YS, 256, 256), BF), V((YS, 256, 256), BF),
            mat(BF), mat(BF), mat(F32), mat(F32),
            V((32, 16, 128), BF), V((32, 16, 128), BF), V((32, 16, 128), BF), V((32, 16, 128), F32),
            V((XS * YS - 1, 2, 16, 128), BF), V((ZS, 2, 16, 128), BF), V((2, 32, 16, 128), BF),
            V((YS - 1, 256, 256), BF), V((YS - 1, 256, 256), BF),
            dma((15,)), dma((5,)), dma((YS - 1,)), dma((YS - 1,)), dma((2,)), dma((2,)), dma((2,)), dma((2,)),
            dma((YS - 1,)), dma((YS - 1,)), dma((39,)), dma((39,)),
        ],
        compiler_params=pltpu.CompilerParams(
            collective_id=0, has_side_effects=True, vmem_limit_bytes=62 * 1024 * 1024),
    )(
        feats[0, 0], w_self, w_neigh, block_vals[0, 0], block_dst[0], block_src[0], block_count,
        prev_partial[0, 0], jnp.swapaxes(mirror_rows[0, 0], 0, 1), send_count[0], jnp.swapaxes(master_rows[0, 0], 0, 1),
        momentum[0, 0], cotangent[0, 0], prev_grad[0, 0], grad_momentum[0, 0],
    )
    hidden, fgrad, sp, sg, wg = pl.pallas_call(
        hand_over,
        out_shape=tuple(sds(r.shape, r.dtype) for r in results[:4]) + (sds((2, 256, 256), F32),),
        in_specs=[hbm] * 5,
        out_specs=[hbm] * 5,
        scratch_shapes=[V(r.shape, r.dtype) for r in results] + [V((2, 256, 256), F32), dma((10,))],
        compiler_params=pltpu.CompilerParams(vmem_limit_bytes=62 * 1024 * 1024),
    )(*results)
    return hidden[None, None], fgrad[None, None], sp[None, None], sg[None, None], wg


def solution(mesh):
    gs = lambda n: P("graph", "slab", *([None] * n))
    in_specs = (
        gs(2), P(), P(), gs(3), gs(1), gs(1), gs(0), gs(2), gs(2), gs(1), gs(2), gs(2), gs(2), gs(2), gs(2),
    )
    out_specs = (gs(2), gs(2), gs(2), gs(2), P())
    return jax.shard_map(shards, mesh=mesh, in_specs=in_specs, out_specs=out_specs, check_vma=False)
```

```python
import functools

import jax
import jax.numpy as jnp
from jax import lax
from jax.experimental import pallas as pl
from jax.experimental.pallas import tpu as pltpu
from jax.sharding import PartitionSpec as P

SMOOTHING = 0.7
MESH = pl.DeviceIdType.MESH
XS, ZS, CORES, YS = 4, 8, 2, 4
N_GRAPH = XS * ZS * CORES
CHIPS = XS * ZS
BF = jnp.bfloat16
F32 = jnp.float32
I32 = jnp.int32


def dot(a, b):
    return lax.dot_general(a, b, (((1,), (0,)), ((), ())), preferred_element_type=F32)


def dot_tn(a, b):
    return lax.dot_general(a, b, (((0,), (0,)), ((), ())), preferred_element_type=F32)


def dot_nt(a, b):
    return lax.dot_general(a, b, (((1,), (1,)), ((), ())), preferred_element_type=F32)


def kernel(
    feats, w_self, w_neigh, vals_h, dst_h, src_h, count_h, pp_h, mir_h, cnt_h, mas_h, mom_h, cot_h, pg_h, gmom_h,
    hidden_o, fgrad_o, sp_o, sg_o, wg_o,
    group, ws, wn, vals, pp, pg, mom, cot, gmom, mir, mas, cnt, dst, src, count,
    msgf, msg, inbox, a_hi, a_lo, at_hi, at_lo,
    hid_v, fg_v, sp_v, sg_v,
    s_a, r_a, s_b, acc_a, r_b, r_c, wfin, s_rs, r_rs,
    lsem, osem, ag_s, ag_r, a2a_s, a2a_r, fw_s, fw_r, rs_s, rs_r, w_s, w_r,
):
    g = lax.axis_index("graph")
    y = lax.axis_index("slab")
    core = g % 2
    chip = g // 2
    z = chip % ZS
    x = chip // ZS
    sibling = (g + 1 - 2 * core, y)
    def near(d, n):
        return min(d, n - d)

    plane = [(dx, dy) for dx in range(XS) for dy in range(YS) if dx or dy]
    plane.sort(key=lambda o: -near(o[0], XS) - near(o[1], YS))
    sheet = [(dx, dz) for dx in range(XS) for dz in range(ZS) if dx or dz]
    sheet.sort(key=lambda o: -near(o[0], XS) - near(o[1], ZS))
    line = sorted(range(1, ZS), key=lambda d: -near(d, ZS))
    slabs = sorted(range(1, YS), key=lambda d: -near(d, YS))


    def at_plane(dx, dy):
        return ((x + dx) % XS, (y + dy) % YS)

    def device(px, pz, py):
        return ((px * ZS + pz) * 2 + core, py)

    barrier = pltpu.get_barrier_semaphore()

    def greet(peer):
        pl.semaphore_signal(barrier, inc=1, device_id=peer, device_id_type=MESH)

    for dx, dz in sheet:
        greet(device((x + dx) % XS, (z + dz) % ZS, y))
    greet(sibling)
    away = [(dx, dy) for dx, dy in plane if dy]
    for dx, dy in away:
        px, py = at_plane(dx, dy)
        greet(device(px, z, py))

    loads = {}
    for i, (name, s, d) in enumerate([
        ("mir", mir_h, mir), ("cnt", cnt_h, cnt), ("pp", pp_h, pp), ("mas", mas_h, mas), ("pg", pg_h, pg), ("own", feats, group.at[y]), ("vals", vals_h, vals),
        ("ws", w_self, ws), ("wn", w_neigh, wn), ("mom", mom_h, mom), ("gmom", gmom_h, gmom), ("cot", cot_h, cot),
        ("dst", dst_h, dst), ("src", src_h, src), ("count", count_h, count),
    ]):
        loads[name] = pltpu.make_async_copy(s, d, lsem.at[i])
        loads[name].start()

    for name in ("mir", "cnt", "mas"):
        loads[name].wait()
    nk = 4 * N_GRAPH
    cnt_row = jnp.concatenate([cnt[...]] * 4, axis=1)
    slot_row = lax.broadcasted_iota(jnp.int32, (1, nk), 1) // N_GRAPH
    live = slot_row < cnt_row
    mir_row = jnp.concatenate([mir[c : c + 1, :] for c in range(4)], axis=1)
    mas_row = jnp.concatenate([mas[c : c + 1, :] for c in range(4)], axis=1)
    mir_row = jnp.where(live, mir_row, -1)
    rows = lax.broadcasted_iota(jnp.int32, (256, nk), 0)
    s_mir = jnp.where(rows == mir_row, 1.0, 0.0).astype(BF)
    s_mas = jnp.where(rows == mas_row, 1.0, 0.0).astype(BF)

    for t, (name, buf, one) in enumerate([("pp", pp, s_mir), ("pg", pg, s_mas)]):
        loads[name].wait()
        out = dot_tn(one, buf[...])
        for c in range(4):
            for h in range(2):
                msgf[t, pl.ds(h * 4 + c, N_GRAPH, stride=8), :] = out[
                    c * N_GRAPH : (c + 1) * N_GRAPH, h * 128 : (h + 1) * 128
                ]
        msg[t] = msgf[t].reshape(CHIPS, 16, 128).astype(BF)
        inbox[t, chip, core] = msg[t, chip]

    pl.semaphore_wait(barrier, CHIPS + len(away))

    ag = {}
    for d in slabs:
        cp = pltpu.make_async_remote_copy(
            feats, group.at[y], ag_s.at[d - 1], ag_r.at[d - 1],
            device_id=(g, (y + d) % YS), device_id_type=MESH)
        cp.start()
        ag[d] = cp

    for t in range(2):
        for dx, dz in sheet:
            px, pz = (x + dx) % XS, (z + dz) % ZS
            pltpu.make_async_remote_copy(
                msg.at[t, px * ZS + pz], inbox.at[t, chip, core], a2a_s.at[t], a2a_r.at[t],
                device_id=device(px, pz, y), device_id_type=MESH).start()

    def forward(t):
        some = inbox.at[t, pl.ds(0, CHIPS - 1), 0]
        pltpu.make_async_copy(some, some, a2a_r.at[t]).wait()
        cp = pltpu.make_async_remote_copy(
            inbox.at[t, :, core], inbox.at[t, :, core], fw_s.at[t], fw_r.at[t],
            device_id=sibling, device_id_type=MESH)
        cp.start()
        return cp

    def received(t):
        both = inbox[t].astype(F32).reshape(N_GRAPH, 16, 128)
        msgf[t] = jnp.where(core == 0, both[:, :8], both[:, 8:]).reshape(N_GRAPH * 8, 128)
        halves = []
        for h in range(2):
            halves.append(jnp.concatenate(
                [msgf[t, pl.ds(h * 4 + c, N_GRAPH, stride=8), :] for c in range(4)], axis=0))
        return jnp.concatenate(halves, axis=1).astype(BF)

    loads["vals"].wait()
    for name in ("dst", "src", "count"):
        loads[name].wait()
    n_live = count[0, 0]
    cells = []
    for b in range(32):
        cells.append(jnp.where(b < n_live, dst[0, b] * 8 + src[0, b], -1))

    def chunk(r, _):
        row = pl.multiple_of(r * 16, 16)
        acc = [jnp.zeros((16, 128), F32) for _ in range(16)]
        for b in range(32):
            v = vals[b, pl.ds(row, 16), :].astype(F32)
            for k in range(16):
                acc[k] = acc[k] + v * jnp.where(cells[b] == k, 1.0, 0.0)
        for k in range(16):
            dk, m = k // 8, k % 8
            t, col = m // 2, (m % 2) * 128
            hi = acc[k].astype(BF)
            lo = (acc[k] - hi.astype(F32)).astype(BF)
            a_hi[t, pl.ds(pl.multiple_of(dk * 128 + row, 16), 16), col : col + 128] = hi
            a_lo[t, pl.ds(pl.multiple_of(dk * 128 + row, 16), 16), col : col + 128] = lo
        return 0

    lax.fori_loop(0, 8, chunk, 0)

    for t in range(YS):
        at_hi[t] = a_hi[t].T
        at_lo[t] = a_lo[t].T
    loads["own"].wait()
    own = group[y]
    loads["ws"].wait()
    loads["wn"].wait()
    pre = dot(own, ws[...])
    local = dot(a_hi[y], own) + dot(a_lo[y], own)
    fw = [forward(0)]
    for d in slabs[::-1]:
        t = (y + YS - d) % YS
        ag[d].wait_recv()
        tile = group[t]
        local = local + dot(a_hi[t], tile) + dot(a_lo[t], tile)

    loads["mom"].wait()
    loads["cot"].wait()
    fw[0].wait_recv()
    sp = SMOOTHING * mom[...] + (1.0 - SMOOTHING) * dot(s_mas, received(0))
    agg = (local + sp).astype(BF)
    pre = pre + dot(agg, wn[...])
    delta = jnp.where(pre > 0, cot[...], jnp.zeros((), BF))

    def tiles(m, h):
        return m[:, h * 128 : (h + 1) * 128].reshape(16, 16, 128)

    given = dot_tn(jnp.where(core == 0, agg, own), delta)
    for h in range(2):
        s_a[h * 16 : (h + 1) * 16] = tiles(given, h).astype(BF)
    cp_a = pltpu.make_async_remote_copy(
        s_a, r_a, w_s.at[0], w_r.at[0], device_id=sibling, device_id_type=MESH)
    cp_a.start()
    fw.append(forward(1))
    kept = dot_tn(jnp.where(core == 0, own, agg), delta)
    cp_a.wait_recv()
    for h in range(2):
        part = slice(h * 16, (h + 1) * 16)
        total = tiles(kept, h) + r_a[part].astype(F32)
        acc_a[part] = total
        s_b[part] = total.astype(BF)
    ops = [cp_a]

    place = x * YS + y
    hop = []
    for i, (dx, dy) in enumerate(plane):
        px, py = at_plane(dx, dy)
        cp = pltpu.make_async_remote_copy(
            s_b.at[pl.ds((px * YS + py) * 2, 2)], r_b.at[i], w_s.at[1 + i], w_r.at[1 + i],
            device_id=device(px, z, py), device_id_type=MESH)
        cp.start()
        hop.append(cp)

    sp_v[...] = sp
    outs = [pltpu.make_async_copy(sp_v, sp_o, osem.at[0])]
    outs[-1].start()
    hid_v[...] = jnp.maximum(pre, 0.0).astype(BF)
    outs.append(pltpu.make_async_copy(hid_v, hidden_o, osem.at[1]))
    outs[-1].start()
    loads["gmom"].wait()
    fw[1].wait_recv()
    sg = SMOOTHING * gmom[...] + (1.0 - SMOOTHING) * dot(s_mir, received(1))
    sg_v[...] = sg
    outs.append(pltpu.make_async_copy(sg_v, sg_o, osem.at[2]))
    outs[-1].start()
    gagg = (dot_nt(delta, wn[...]) + sg).astype(BF)
    rs = []
    for d in slabs:
        t = (y + d) % YS
        s_rs[d - 1] = (dot(at_hi[t], gagg) + dot(at_lo[t], gagg)).astype(BF)
        cp = pltpu.make_async_remote_copy(
            s_rs.at[d - 1], r_rs.at[d - 1], rs_s.at[d - 1], rs_r.at[d - 1],
            device_id=(g, t), device_id_type=MESH)
        cp.start()
        rs.append(cp)

    for cp in hop:
        cp.wait_recv()
    ops += hop
    total = acc_a[pl.ds(place * 2, 2)]
    for i in range(len(plane)):
        total = total + r_b[i].astype(F32)

    r_c[z] = total.astype(BF)
    hop = []
    for d in line:
        cp = pltpu.make_async_remote_copy(
            r_c.at[z], r_c.at[z], w_s.at[15 + d], w_r.at[15 + d],
            device_id=device(x, (z + d) % ZS, y), device_id_type=MESH)
        cp.start()
        hop.append(cp)
    fg = dot_nt(delta, ws[...]) + dot(at_hi[y], gagg) + dot(at_lo[y], gagg)
    for cp in hop:
        cp.wait_recv()
    ops += hop
    total = r_c[0].astype(F32)
    for i in range(1, ZS):
        total = total + r_c[i].astype(F32)
    mine = wfin.at[core, pl.ds(place * 2, 2)]
    mine[...] = total.astype(BF)

    hop = []
    for i, (dx, dy) in enumerate(plane):
        px, py = at_plane(dx, dy)
        cp = pltpu.make_async_remote_copy(
            mine, mine, w_s.at[23 + i], w_r.at[23 + i], device_id=device(px, z, py), device_id_type=MESH)
        cp.start()
        hop.append(cp)
    for cp in rs:
        cp.wait_recv()
    for d in range(1, YS):
        fg = fg + r_rs[d - 1].astype(F32)
    fg_v[...] = fg.astype(BF)
    outs.append(pltpu.make_async_copy(fg_v, fgrad_o, osem.at[3]))
    outs[-1].start()

    for cp in hop:
        cp.wait_recv()
    ops += hop
    last = pltpu.make_async_remote_copy(
        wfin.at[core], wg_o.at[core], w_s.at[38], w_r.at[38], device_id=sibling, device_id_type=MESH)
    last.start()
    ops.append(last)
    outs.append(pltpu.make_async_copy(wfin.at[core], wg_o.at[core], osem.at[4]))
    outs[-1].start()
    last.wait_recv()

    for cp in list(ag.values()) + fw + rs + ops:
        cp.wait_send()
    for t in range(2):
        some = msg.at[t, pl.ds(0, CHIPS - 1)]
        pltpu.make_async_copy(some, some, a2a_s.at[t]).wait()
    for cp in outs:
        cp.wait()


def hand_over(*refs):
    results, outs, stage, wide, sem = refs[:5], refs[5:10], refs[10:15], refs[15], refs[16]
    order = (4, 2, 3, 0, 1)
    pull = [pltpu.make_async_copy(results[i], stage[i], sem.at[i]) for i in range(5)]
    push = [pltpu.make_async_copy(wide if i == 4 else stage[i], outs[i], sem.at[5 + i]) for i in range(5)]
    for i in order:
        pull[i].start()
    for i in order:
        pull[i].wait()
        if i == 4:
            scale = 1.0 / (N_GRAPH * YS * 256) ** 0.5
            for k in range(2):
                for h in range(2):
                    wide[k, :, h * 128 : (h + 1) * 128] = (
                        stage[4][k, h * 16 : (h + 1) * 16].astype(F32).reshape(256, 128) * scale)
        push[i].start()
    for i in order:
        push[i].wait()


def shards(
    feats, w_self, w_neigh, block_vals, block_dst, block_src, block_count, prev_partial,
    mirror_rows, send_count, master_rows, momentum, cotangent, prev_grad, grad_momentum,
):
    sds = jax.ShapeDtypeStruct
    hbm = pl.BlockSpec(memory_space=pl.ANY)
    V, S = pltpu.VMEM, pltpu.SMEM
    dma = pltpu.SemaphoreType.DMA
    mat = lambda dt: V((256, 256), dt)
    results = pl.pallas_call(
        kernel,
        out_shape=(
            sds((256, 256), BF), sds((256, 256), BF), sds((256, 256), F32), sds((256, 256), F32),
            sds((2, 32, 16, 128), BF),
        ),
        in_specs=[hbm] * 15,
        out_specs=[hbm] * 5,
        scratch_shapes=[
            V((YS, 256, 256), BF), mat(BF), mat(BF), V((32, 128, 128), BF), mat(BF), mat(BF), mat(F32), mat(BF), mat(F32),
            V((4, N_GRAPH), I32), V((4, N_GRAPH), I32), V((1, N_GRAPH), I32), S((1, 32), I32), S((1, 32), I32), S((1, 1), I32),
            V((2, N_GRAPH * 8, 128), F32), V((2, CHIPS, 16, 128), BF), V((2, CHIPS, CORES, 16, 128), BF),
            V((YS, 256, 256), BF), V((YS, 256, 256), BF), V((YS, 256, 256), BF), V((YS, 256, 256), BF),
            mat(BF), mat(BF), mat(F32), mat(F32),
            V((32, 16, 128), BF), V((32, 16, 128), BF), V((32, 16, 128), BF), V((32, 16, 128), F32),
            V((XS * YS - 1, 2, 16, 128), BF), V((ZS, 2, 16, 128), BF), V((2, 32, 16, 128), BF),
            V((YS - 1, 256, 256), BF), V((YS - 1, 256, 256), BF),
            dma((15,)), dma((5,)), dma((YS - 1,)), dma((YS - 1,)), dma((2,)), dma((2,)), dma((2,)), dma((2,)),
            dma((YS - 1,)), dma((YS - 1,)), dma((39,)), dma((39,)),
        ],
        compiler_params=pltpu.CompilerParams(
            collective_id=0, has_side_effects=True, vmem_limit_bytes=62 * 1024 * 1024),
    )(
        feats[0, 0], w_self, w_neigh, block_vals[0, 0], block_dst[0], block_src[0], block_count,
        prev_partial[0, 0], jnp.swapaxes(mirror_rows[0, 0], 0, 1), send_count[0], jnp.swapaxes(master_rows[0, 0], 0, 1),
        momentum[0, 0], cotangent[0, 0], prev_grad[0, 0], grad_momentum[0, 0],
    )
    hidden, fgrad, sp, sg, wg = pl.pallas_call(
        hand_over,
        out_shape=tuple(sds(r.shape, r.dtype) for r in results[:4]) + (sds((2, 256, 256), F32),),
        in_specs=[hbm] * 5,
        out_specs=[hbm] * 5,
        scratch_shapes=[V(r.shape, r.dtype) for r in results] + [V((2, 256, 256), F32), dma((10,))],
        compiler_params=pltpu.CompilerParams(vmem_limit_bytes=62 * 1024 * 1024),
    )(*results)
    return hidden[None, None], fgrad[None, None], sp[None, None], sg[None, None], wg


def solution(mesh):
    gs = lambda n: P("graph", "slab", *([None] * n))
    in_specs = (
        gs(2), P(), P(), gs(3), gs(1), gs(1), gs(0), gs(2), gs(2), gs(1), gs(2), gs(2), gs(2), gs(2), gs(2),
    )
    out_specs = (gs(2), gs(2), gs(2), gs(2), P())
    return jax.shard_map(shards, mesh=mesh, in_specs=in_specs, out_specs=out_specs, check_vma=False)
```

```python
import functools

import jax
import jax.numpy as jnp
from jax import lax
from jax.experimental import pallas as pl
from jax.experimental.pallas import tpu as pltpu
from jax.sharding import PartitionSpec as P

SMOOTHING = 0.7
MESH = pl.DeviceIdType.MESH
XS, ZS, CORES, YS = 4, 8, 2, 4
N_GRAPH = XS * ZS * CORES
CHIPS = XS * ZS
BF = jnp.bfloat16
F32 = jnp.float32
I32 = jnp.int32


def dot(a, b):
    return lax.dot_general(a, b, (((1,), (0,)), ((), ())), preferred_element_type=F32)


def dot_tn(a, b):
    return lax.dot_general(a, b, (((0,), (0,)), ((), ())), preferred_element_type=F32)


def dot_nt(a, b):
    return lax.dot_general(a, b, (((1,), (1,)), ((), ())), preferred_element_type=F32)


def kernel(
    feats, w_self, w_neigh, vals_h, dst_h, src_h, count_h, pp_h, mir_h, cnt_h, mas_h, mom_h, cot_h, pg_h, gmom_h,
    hidden_o, fgrad_o, sp_o, sg_o, wfin,
    group, ws, wn, vals, pp, pg, mom, cot, gmom, mir, mas, cnt, dst, src, count,
    msgf, msg, inbox, a_hi, a_lo, at_hi, at_lo,
    s_a, r_a, s_b, acc_a, r_b, r_c, s_rs, r_rs,
    lsem, ag_s, ag_r, a2a_s, a2a_r, fw_s, fw_r, rs_s, rs_r, w_s, w_r,
):
    g = lax.axis_index("graph")
    y = lax.axis_index("slab")
    core = g % 2
    chip = g // 2
    z = chip % ZS
    x = chip // ZS
    sibling = (g + 1 - 2 * core, y)
    def near(d, n):
        return min(d, n - d)

    plane = [(dx, dy) for dx in range(XS) for dy in range(YS) if dx or dy]
    plane.sort(key=lambda o: -near(o[0], XS) - near(o[1], YS))
    sheet = [(dx, dz) for dx in range(XS) for dz in range(ZS) if dx or dz]
    sheet.sort(key=lambda o: -near(o[0], XS) - near(o[1], ZS))
    line = sorted(range(1, ZS), key=lambda d: -near(d, ZS))
    slabs = sorted(range(1, YS), key=lambda d: -near(d, YS))


    def at_plane(dx, dy):
        return ((x + dx) % XS, (y + dy) % YS)

    def device(px, pz, py):
        return ((px * ZS + pz) * 2 + core, py)

    barrier = pltpu.get_barrier_semaphore()

    def greet(peer):
        pl.semaphore_signal(barrier, inc=1, device_id=peer, device_id_type=MESH)

    for dx, dz in sheet:
        greet(device((x + dx) % XS, (z + dz) % ZS, y))
    greet(sibling)
    away = [(dx, dy) for dx, dy in plane if dy]
    for dx, dy in away:
        px, py = at_plane(dx, dy)
        greet(device(px, z, py))

    loads = {}
    for i, (name, s, d) in enumerate([
        ("mir", mir_h, mir), ("cnt", cnt_h, cnt), ("pp", pp_h, pp), ("mas", mas_h, mas), ("pg", pg_h, pg), ("own", feats, group.at[y]), ("vals", vals_h, vals),
        ("ws", w_self, ws), ("wn", w_neigh, wn), ("mom", mom_h, mom), ("gmom", gmom_h, gmom), ("cot", cot_h, cot),
        ("dst", dst_h, dst), ("src", src_h, src), ("count", count_h, count),
    ]):
        loads[name] = pltpu.make_async_copy(s, d, lsem.at[i])
        loads[name].start()

    for name in ("mir", "cnt", "mas"):
        loads[name].wait()
    nk = 4 * N_GRAPH
    cnt_row = jnp.concatenate([cnt[...]] * 4, axis=1)
    slot_row = lax.broadcasted_iota(jnp.int32, (1, nk), 1) // N_GRAPH
    live = slot_row < cnt_row
    mir_row = jnp.concatenate([mir[c : c + 1, :] for c in range(4)], axis=1)
    mas_row = jnp.concatenate([mas[c : c + 1, :] for c in range(4)], axis=1)
    mir_row = jnp.where(live, mir_row, -1)
    rows = lax.broadcasted_iota(jnp.int32, (256, nk), 0)
    s_mir = jnp.where(rows == mir_row, 1.0, 0.0).astype(BF)
    s_mas = jnp.where(rows == mas_row, 1.0, 0.0).astype(BF)

    for t, (name, buf, one) in enumerate([("pp", pp, s_mir), ("pg", pg, s_mas)]):
        loads[name].wait()
        out = dot_tn(one, buf[...])
        for c in range(4):
            for h in range(2):
                msgf[t, pl.ds(h * 4 + c, N_GRAPH, stride=8), :] = out[
                    c * N_GRAPH : (c + 1) * N_GRAPH, h * 128 : (h + 1) * 128
                ]
        msg[t] = msgf[t].reshape(CHIPS, 16, 128).astype(BF)
        inbox[t, chip, core] = msg[t, chip]

    pl.semaphore_wait(barrier, CHIPS + len(away))

    ag = {}
    for d in slabs:
        cp = pltpu.make_async_remote_copy(
            feats, group.at[y], ag_s.at[d - 1], ag_r.at[d - 1],
            device_id=(g, (y + d) % YS), device_id_type=MESH)
        cp.start()
        ag[d] = cp

    for t in range(2):
        for dx, dz in sheet:
            px, pz = (x + dx) % XS, (z + dz) % ZS
            pltpu.make_async_remote_copy(
                msg.at[t, px * ZS + pz], inbox.at[t, chip, core], a2a_s.at[t], a2a_r.at[t],
                device_id=device(px, pz, y), device_id_type=MESH).start()

    def forward(t):
        some = inbox.at[t, pl.ds(0, CHIPS - 1), 0]
        pltpu.make_async_copy(some, some, a2a_r.at[t]).wait()
        cp = pltpu.make_async_remote_copy(
            inbox.at[t, :, core], inbox.at[t, :, core], fw_s.at[t], fw_r.at[t],
            device_id=sibling, device_id_type=MESH)
        cp.start()
        return cp

    def received(t):
        both = inbox[t].astype(F32).reshape(N_GRAPH, 16, 128)
        msgf[t] = jnp.where(core == 0, both[:, :8], both[:, 8:]).reshape(N_GRAPH * 8, 128)
        halves = []
        for h in range(2):
            halves.append(jnp.concatenate(
                [msgf[t, pl.ds(h * 4 + c, N_GRAPH, stride=8), :] for c in range(4)], axis=0))
        return jnp.concatenate(halves, axis=1).astype(BF)

    loads["vals"].wait()
    for name in ("dst", "src", "count"):
        loads[name].wait()
    n_live = count[0, 0]
    cells = []
    for b in range(32):
        cells.append(jnp.where(b < n_live, dst[0, b] * 8 + src[0, b], -1))

    def chunk(r, _):
        row = pl.multiple_of(r * 16, 16)
        acc = [jnp.zeros((16, 128), F32) for _ in range(16)]
        for b in range(32):
            v = vals[b, pl.ds(row, 16), :].astype(F32)
            for k in range(16):
                acc[k] = acc[k] + v * jnp.where(cells[b] == k, 1.0, 0.0)
        for k in range(16):
            dk, m = k // 8, k % 8
            t, col = m // 2, (m % 2) * 128
            hi = acc[k].astype(BF)
            lo = (acc[k] - hi.astype(F32)).astype(BF)
            a_hi[t, pl.ds(pl.multiple_of(dk * 128 + row, 16), 16), col : col + 128] = hi
            a_lo[t, pl.ds(pl.multiple_of(dk * 128 + row, 16), 16), col : col + 128] = lo
        return 0

    lax.fori_loop(0, 8, chunk, 0)

    for t in range(YS):
        at_hi[t] = a_hi[t].T
        at_lo[t] = a_lo[t].T
    loads["own"].wait()
    own = group[y]
    loads["ws"].wait()
    loads["wn"].wait()
    pre = dot(own, ws[...])
    local = dot(a_hi[y], own) + dot(a_lo[y], own)
    fw = [forward(0)]
    for d in slabs[::-1]:
        t = (y + YS - d) % YS
        ag[d].wait_recv()
        tile = group[t]
        local = local + dot(a_hi[t], tile) + dot(a_lo[t], tile)

    loads["mom"].wait()
    loads["cot"].wait()
    fw[0].wait_recv()
    sp = SMOOTHING * mom[...] + (1.0 - SMOOTHING) * dot(s_mas, received(0))
    agg = (local + sp).astype(BF)
    pre = pre + dot(agg, wn[...])
    delta = jnp.where(pre > 0, cot[...], jnp.zeros((), BF))

    def tiles(m, h):
        return m[:, h * 128 : (h + 1) * 128].reshape(16, 16, 128)

    given = dot_tn(jnp.where(core == 0, agg, own), delta)
    for h in range(2):
        s_a[h * 16 : (h + 1) * 16] = tiles(given, h).astype(BF)
    cp_a = pltpu.make_async_remote_copy(
        s_a, r_a, w_s.at[0], w_r.at[0], device_id=sibling, device_id_type=MESH)
    cp_a.start()
    fw.append(forward(1))
    kept = dot_tn(jnp.where(core == 0, own, agg), delta)
    cp_a.wait_recv()
    for h in range(2):
        part = slice(h * 16, (h + 1) * 16)
        total = tiles(kept, h) + r_a[part].astype(F32)
        acc_a[part] = total
        s_b[part] = total.astype(BF)
    ops = [cp_a]

    place = x * YS + y
    hop = []
    for i, (dx, dy) in enumerate(plane):
        px, py = at_plane(dx, dy)
        cp = pltpu.make_async_remote_copy(
            s_b.at[pl.ds((px * YS + py) * 2, 2)], r_b.at[i], w_s.at[1 + i], w_r.at[1 + i],
            device_id=device(px, z, py), device_id_type=MESH)
        cp.start()
        hop.append(cp)

    sp_o[...] = sp
    hidden_o[...] = jnp.maximum(pre, 0.0).astype(BF)
    loads["gmom"].wait()
    fw[1].wait_recv()
    sg = SMOOTHING * gmom[...] + (1.0 - SMOOTHING) * dot(s_mir, received(1))
    sg_o[...] = sg
    gagg = (dot_nt(delta, wn[...]) + sg).astype(BF)
    rs = []
    for d in slabs:
        t = (y + d) % YS
        s_rs[d - 1] = (dot(at_hi[t], gagg) + dot(at_lo[t], gagg)).astype(BF)
        cp = pltpu.make_async_remote_copy(
            s_rs.at[d - 1], r_rs.at[d - 1], rs_s.at[d - 1], rs_r.at[d - 1],
            device_id=(g, t), device_id_type=MESH)
        cp.start()
        rs.append(cp)

    for cp in hop:
        cp.wait_recv()
    ops += hop
    total = acc_a[pl.ds(place * 2, 2)]
    for i in range(len(plane)):
        total = total + r_b[i].astype(F32)

    r_c[z] = total.astype(BF)
    hop = []
    for d in line:
        cp = pltpu.make_async_remote_copy(
            r_c.at[z], r_c.at[z], w_s.at[15 + d], w_r.at[15 + d],
            device_id=device(x, (z + d) % ZS, y), device_id_type=MESH)
        cp.start()
        hop.append(cp)
    fg = dot_nt(delta, ws[...]) + dot(at_hi[y], gagg) + dot(at_lo[y], gagg)
    for cp in hop:
        cp.wait_recv()
    ops += hop
    total = r_c[0].astype(F32)
    for i in range(1, ZS):
        total = total + r_c[i].astype(F32)
    mine = wfin.at[core, pl.ds(place * 2, 2)]
    mine[...] = total.astype(BF)

    hop = []
    for i, (dx, dy) in enumerate(plane):
        px, py = at_plane(dx, dy)
        cp = pltpu.make_async_remote_copy(
            mine, mine, w_s.at[23 + i], w_r.at[23 + i], device_id=device(px, z, py), device_id_type=MESH)
        cp.start()
        hop.append(cp)
    for cp in rs:
        cp.wait_recv()
    for d in range(1, YS):
        fg = fg + r_rs[d - 1].astype(F32)
    fgrad_o[...] = fg.astype(BF)

    for cp in hop:
        cp.wait_recv()
    ops += hop
    last = pltpu.make_async_remote_copy(
        wfin.at[core], wfin.at[core], w_s.at[38], w_r.at[38], device_id=sibling, device_id_type=MESH)
    last.start()
    ops.append(last)
    last.wait_recv()

    for cp in list(ag.values()) + fw + rs + ops:
        cp.wait_send()
    for t in range(2):
        some = msg.at[t, pl.ds(0, CHIPS - 1)]
        pltpu.make_async_copy(some, some, a2a_s.at[t]).wait()


def hand_over(*refs):
    results, outs, wide, sem = refs[:5], refs[5:10], refs[10], refs[11]
    push = [pltpu.make_async_copy(results[i] if i < 4 else wide, outs[i], sem.at[i]) for i in range(5)]
    for i in (2, 3, 0, 1):
        push[i].start()
    scale = 1.0 / (N_GRAPH * YS * 256) ** 0.5
    for k in range(2):
        for h in range(2):
            wide[k, :, h * 128 : (h + 1) * 128] = (
                results[4][k, h * 16 : (h + 1) * 16].astype(F32).reshape(256, 128) * scale)
    push[4].start()
    for cp in push:
        cp.wait()


def shards(
    feats, w_self, w_neigh, block_vals, block_dst, block_src, block_count, prev_partial,
    mirror_rows, send_count, master_rows, momentum, cotangent, prev_grad, grad_momentum,
):
    sds = jax.ShapeDtypeStruct
    hbm = pl.BlockSpec(memory_space=pl.ANY)
    vm = pl.BlockSpec(memory_space=pltpu.VMEM)
    V, S = pltpu.VMEM, pltpu.SMEM
    dma = pltpu.SemaphoreType.DMA
    mat = lambda dt: V((256, 256), dt)
    results = pl.pallas_call(
        kernel,
        out_shape=(
            mat(BF), mat(BF), mat(F32), mat(F32), V((2, 32, 16, 128), BF),
        ),
        in_specs=[hbm] * 15,
        out_specs=[vm] * 5,
        scratch_shapes=[
            V((YS, 256, 256), BF), mat(BF), mat(BF), V((32, 128, 128), BF), mat(BF), mat(BF), mat(F32), mat(BF), mat(F32),
            V((4, N_GRAPH), I32), V((4, N_GRAPH), I32), V((1, N_GRAPH), I32), S((1, 32), I32), S((1, 32), I32), S((1, 1), I32),
            V((2, N_GRAPH * 8, 128), F32), V((2, CHIPS, 16, 128), BF), V((2, CHIPS, CORES, 16, 128), BF),
            V((YS, 256, 256), BF), V((YS, 256, 256), BF), V((YS, 256, 256), BF), V((YS, 256, 256), BF),
            V((32, 16, 128), BF), V((32, 16, 128), BF), V((32, 16, 128), BF), V((32, 16, 128), F32),
            V((XS * YS - 1, 2, 16, 128), BF), V((ZS, 2, 16, 128), BF),
            V((YS - 1, 256, 256), BF), V((YS - 1, 256, 256), BF),
            dma((15,)), dma((YS - 1,)), dma((YS - 1,)), dma((2,)), dma((2,)), dma((2,)), dma((2,)),
            dma((YS - 1,)), dma((YS - 1,)), dma((39,)), dma((39,)),
        ],
        compiler_params=pltpu.CompilerParams(
            collective_id=0, has_side_effects=True, vmem_limit_bytes=24 * 1024 * 1024),
    )(*[a if a.size == 1 else pltpu.with_memory_space_constraint(a, pltpu.HBM) for a in (
        feats[0, 0], w_self, w_neigh, block_vals[0, 0], block_dst[0], block_src[0], block_count,
        prev_partial[0, 0], jnp.swapaxes(mirror_rows[0, 0], 0, 1), send_count[0], jnp.swapaxes(master_rows[0, 0], 0, 1),
        momentum[0, 0], cotangent[0, 0], prev_grad[0, 0], grad_momentum[0, 0],
    )])
    hidden, fgrad, sp, sg, wg = pl.pallas_call(
        hand_over,
        out_shape=tuple(sds(r.shape, r.dtype) for r in results[:4]) + (sds((2, 256, 256), F32),),
        in_specs=[vm] * 5,
        out_specs=[hbm] * 5,
        scratch_shapes=[V((2, 256, 256), F32), dma((5,))],
        compiler_params=pltpu.CompilerParams(vmem_limit_bytes=24 * 1024 * 1024),
    )(*results)
    return hidden[None, None], fgrad[None, None], sp[None, None], sg[None, None], wg


def solution(mesh):
    gs = lambda n: P("graph", "slab", *([None] * n))
    in_specs = (
        gs(2), P(), P(), gs(3), gs(1), gs(1), gs(0), gs(2), gs(2), gs(1), gs(2), gs(2), gs(2), gs(2), gs(2),
    )
    out_specs = (gs(2), gs(2), gs(2), gs(2), P())
    return jax.shard_map(shards, mesh=mesh, in_specs=in_specs, out_specs=out_specs, check_vma=False)
```

```python
import functools

import jax
import jax.numpy as jnp
from jax import lax
from jax.experimental import pallas as pl
from jax.experimental.pallas import tpu as pltpu
from jax.sharding import PartitionSpec as P

SMOOTHING = 0.7
MESH = pl.DeviceIdType.MESH
XS, ZS, CORES, YS = 4, 8, 2, 4
N_GRAPH = XS * ZS * CORES
CHIPS = XS * ZS
BF = jnp.bfloat16
F32 = jnp.float32
I32 = jnp.int32


def dot(a, b):
    return lax.dot_general(a, b, (((1,), (0,)), ((), ())), preferred_element_type=F32)


def dot_tn(a, b):
    return lax.dot_general(a, b, (((0,), (0,)), ((), ())), preferred_element_type=F32)


def dot_nt(a, b):
    return lax.dot_general(a, b, (((1,), (1,)), ((), ())), preferred_element_type=F32)


def kernel(
    feats, w_self, w_neigh, vals_h, dst_h, src_h, count_h, pp_h, mir_h, cnt_h, mas_h, mom_h, cot_h, pg_h, gmom_h,
    hidden_o, fgrad_o, sp_o, sg_o, wfin,
    group, ws, wn, vals, pp, pg, mom, cot, gmom, mir, mas, cnt, dst, src, count,
    msgf, msg, inbox, a_hi, a_lo, at_hi, at_lo,
    s_a, r_a, s_b, acc_a, r_b, r_c, s_rs, r_rs,
    lsem, ag_s, ag_r, a2a_s, a2a_r, fw_s, fw_r, rs_s, rs_r, w_s, w_r,
):
    g = lax.axis_index("graph")
    y = lax.axis_index("slab")
    core = g % 2
    chip = g // 2
    z = chip % ZS
    x = chip // ZS
    sibling = (g + 1 - 2 * core, y)
    def near(d, n):
        return min(d, n - d)

    plane = [(dx, dy) for dx in range(XS) for dy in range(YS) if dx or dy]
    plane.sort(key=lambda o: -near(o[0], XS) - near(o[1], YS))
    sheet = [(dx, dz) for dx in range(XS) for dz in range(ZS) if dx or dz]
    sheet.sort(key=lambda o: -near(o[0], XS) - near(o[1], ZS))
    line = sorted(range(1, ZS), key=lambda d: -near(d, ZS))
    slabs = sorted(range(1, YS), key=lambda d: -near(d, YS))


    def at_plane(dx, dy):
        return ((x + dx) % XS, (y + dy) % YS)

    def device(px, pz, py):
        return ((px * ZS + pz) * 2 + core, py)

    barrier = pltpu.get_barrier_semaphore()

    def greet(peer):
        pl.semaphore_signal(barrier, inc=1, device_id=peer, device_id_type=MESH)

    for dx, dz in sheet:
        greet(device((x + dx) % XS, (z + dz) % ZS, y))
    greet(sibling)
    away = [(dx, dy) for dx, dy in plane if dy]
    for dx, dy in away:
        px, py = at_plane(dx, dy)
        greet(device(px, z, py))

    loads = {}
    for i, (name, s, d) in enumerate([
        ("mir", mir_h, mir), ("cnt", cnt_h, cnt), ("pp", pp_h, pp), ("mas", mas_h, mas), ("pg", pg_h, pg), ("own", feats, group.at[y]), ("vals", vals_h, vals),
        ("ws", w_self, ws), ("wn", w_neigh, wn), ("mom", mom_h, mom), ("gmom", gmom_h, gmom), ("cot", cot_h, cot),
        ("dst", dst_h, dst), ("src", src_h, src), ("count", count_h, count),
    ]):
        loads[name] = pltpu.make_async_copy(s, d, lsem.at[i])
        loads[name].start()

    for name in ("mir", "cnt", "mas"):
        loads[name].wait()
    nk = 4 * N_GRAPH
    cnt_row = jnp.concatenate([cnt[...]] * 4, axis=1)
    slot_row = lax.broadcasted_iota(jnp.int32, (1, nk), 1) // N_GRAPH
    live = slot_row < cnt_row
    mir_row = jnp.concatenate([mir[c : c + 1, :] for c in range(4)], axis=1)
    mas_row = jnp.concatenate([mas[c : c + 1, :] for c in range(4)], axis=1)
    mir_row = jnp.where(live, mir_row, -1)
    rows = lax.broadcasted_iota(jnp.int32, (256, nk), 0)
    s_mir = jnp.where(rows == mir_row, 1.0, 0.0).astype(BF)
    s_mas = jnp.where(rows == mas_row, 1.0, 0.0).astype(BF)

    for t, (name, buf, one) in enumerate([("pp", pp, s_mir), ("pg", pg, s_mas)]):
        loads[name].wait()
        out = dot_tn(one, buf[...])
        for c in range(4):
            for h in range(2):
                msgf[t, pl.ds(h * 4 + c, N_GRAPH, stride=8), :] = out[
                    c * N_GRAPH : (c + 1) * N_GRAPH, h * 128 : (h + 1) * 128
                ]
        msg[t] = msgf[t].reshape(CHIPS, 16, 128).astype(BF)
        inbox[t, chip, core] = msg[t, chip]

    pl.semaphore_wait(barrier, CHIPS + len(away))

    loads["own"].wait()
    ag = {}
    for d in slabs:
        cp = pltpu.make_async_remote_copy(
            group.at[y], group.at[y], ag_s.at[d - 1], ag_r.at[d - 1],
            device_id=(g, (y + d) % YS), device_id_type=MESH)
        cp.start()
        ag[d] = cp

    for t in range(2):
        for dx, dz in sheet:
            px, pz = (x + dx) % XS, (z + dz) % ZS
            pltpu.make_async_remote_copy(
                msg.at[t, px * ZS + pz], inbox.at[t, chip, core], a2a_s.at[t], a2a_r.at[t],
                device_id=device(px, pz, y), device_id_type=MESH).start()

    def forward(t):
        some = inbox.at[t, pl.ds(0, CHIPS - 1), 0]
        pltpu.make_async_copy(some, some, a2a_r.at[t]).wait()
        cp = pltpu.make_async_remote_copy(
            inbox.at[t, :, core], inbox.at[t, :, core], fw_s.at[t], fw_r.at[t],
            device_id=sibling, device_id_type=MESH)
        cp.start()
        return cp

    def received(t):
        both = inbox[t].astype(F32).reshape(N_GRAPH, 16, 128)
        msgf[t] = jnp.where(core == 0, both[:, :8], both[:, 8:]).reshape(N_GRAPH * 8, 128)
        halves = []
        for h in range(2):
            halves.append(jnp.concatenate(
                [msgf[t, pl.ds(h * 4 + c, N_GRAPH, stride=8), :] for c in range(4)], axis=0))
        return jnp.concatenate(halves, axis=1).astype(BF)

    loads["vals"].wait()
    for name in ("dst", "src", "count"):
        loads[name].wait()
    n_live = count[0, 0]
    cells = []
    for b in range(32):
        cells.append(jnp.where(b < n_live, dst[0, b] * 8 + src[0, b], -1))

    def chunk(r, _):
        row = pl.multiple_of(r * 16, 16)
        acc = [jnp.zeros((16, 128), F32) for _ in range(16)]
        for b in range(32):
            v = vals[b, pl.ds(row, 16), :].astype(F32)
            for k in range(16):
                acc[k] = acc[k] + v * jnp.where(cells[b] == k, 1.0, 0.0)
        for k in range(16):
            dk, m = k // 8, k % 8
            t, col = m // 2, (m % 2) * 128
            hi = acc[k].astype(BF)
            lo = (acc[k] - hi.astype(F32)).astype(BF)
            a_hi[t, pl.ds(pl.multiple_of(dk * 128 + row, 16), 16), col : col + 128] = hi
            a_lo[t, pl.ds(pl.multiple_of(dk * 128 + row, 16), 16), col : col + 128] = lo
        return 0

    lax.fori_loop(0, 8, chunk, 0)

    for t in range(YS):
        at_hi[t] = a_hi[t].T
        at_lo[t] = a_lo[t].T
    own = group[y]
    loads["ws"].wait()
    loads["wn"].wait()
    pre = dot(own, ws[...])
    local = dot(a_hi[y], own) + dot(a_lo[y], own)
    fw = [forward(0)]
    for d in slabs[::-1]:
        t = (y + YS - d) % YS
        ag[d].wait_recv()
        tile = group[t]
        local = local + dot(a_hi[t], tile) + dot(a_lo[t], tile)

    loads["mom"].wait()
    loads["cot"].wait()
    fw[0].wait_recv()
    sp = SMOOTHING * mom[...] + (1.0 - SMOOTHING) * dot(s_mas, received(0))
    agg = (local + sp).astype(BF)
    pre = pre + dot(agg, wn[...])
    delta = jnp.where(pre > 0, cot[...], jnp.zeros((), BF))

    def tiles(m, h):
        return m[:, h * 128 : (h + 1) * 128].reshape(16, 16, 128)

    ops = []
    lhs = jnp.where(core == 0, agg, own)
    for h in range(2):
        part = pl.ds(h * 16, 16)
        s_a[part] = dot_tn(lhs, delta[:, h * 128 : (h + 1) * 128]).reshape(16, 16, 128).astype(BF)
        cp = pltpu.make_async_remote_copy(
            s_a.at[part], r_a.at[part], w_s.at[39 * h], w_r.at[39 * h], device_id=sibling, device_id_type=MESH)
        cp.start()
        ops.append(cp)
    kept = dot_tn(jnp.where(core == 0, own, agg), delta)
    for h in range(2):
        ops[h].wait_recv()
        part = slice(h * 16, (h + 1) * 16)
        total = tiles(kept, h) + r_a[part].astype(F32)
        acc_a[part] = total
        s_b[part] = total.astype(BF)

    place = x * YS + y
    hop = []
    for i, (dx, dy) in enumerate(plane):
        px, py = at_plane(dx, dy)
        cp = pltpu.make_async_remote_copy(
            s_b.at[pl.ds((px * YS + py) * 2, 2)], r_b.at[i], w_s.at[1 + i], w_r.at[1 + i],
            device_id=device(px, z, py), device_id_type=MESH)
        cp.start()
        hop.append(cp)

    fw.append(forward(1))
    sp_o[...] = sp
    hidden_o[...] = jnp.maximum(pre, 0.0).astype(BF)
    loads["gmom"].wait()
    fw[1].wait_recv()
    sg = SMOOTHING * gmom[...] + (1.0 - SMOOTHING) * dot(s_mir, received(1))
    sg_o[...] = sg
    gagg = (dot_nt(delta, wn[...]) + sg).astype(BF)
    rs = []
    for d in slabs:
        t = (y + d) % YS
        s_rs[d - 1] = (dot(at_hi[t], gagg) + dot(at_lo[t], gagg)).astype(BF)
        cp = pltpu.make_async_remote_copy(
            s_rs.at[d - 1], r_rs.at[d - 1], rs_s.at[d - 1], rs_r.at[d - 1],
            device_id=(g, t), device_id_type=MESH)
        rs.append(cp)

    for cp in hop:
        cp.wait_recv()
    ops += hop
    total = acc_a[pl.ds(place * 2, 2)]
    for i in range(len(plane)):
        total = total + r_b[i].astype(F32)

    r_c[z] = total.astype(BF)
    hop = []
    for d in line:
        cp = pltpu.make_async_remote_copy(
            r_c.at[z], r_c.at[z], w_s.at[15 + d], w_r.at[15 + d],
            device_id=device(x, (z + d) % ZS, y), device_id_type=MESH)
        cp.start()
        hop.append(cp)
    for cp in rs:
        cp.start()
    fg = dot_nt(delta, ws[...]) + dot(at_hi[y], gagg) + dot(at_lo[y], gagg)
    for cp in hop:
        cp.wait_recv()
    ops += hop
    total = r_c[0].astype(F32)
    for i in range(1, ZS):
        total = total + r_c[i].astype(F32)
    mine = wfin.at[core, pl.ds(place * 2, 2)]
    mine[...] = total.astype(BF)

    hop = []
    for i, (dx, dy) in enumerate(plane):
        px, py = at_plane(dx, dy)
        cp = pltpu.make_async_remote_copy(
            mine, mine, w_s.at[23 + i], w_r.at[23 + i], device_id=device(px, z, py), device_id_type=MESH)
        cp.start()
        hop.append(cp)
    for cp in rs:
        cp.wait_recv()
    for d in range(1, YS):
        fg = fg + r_rs[d - 1].astype(F32)
    fgrad_o[...] = fg.astype(BF)

    for cp in hop:
        cp.wait_recv()
    ops += hop
    last = pltpu.make_async_remote_copy(
        wfin.at[core], wfin.at[core], w_s.at[38], w_r.at[38], device_id=sibling, device_id_type=MESH)
    last.start()
    ops.append(last)
    last.wait_recv()

    for cp in list(ag.values()) + fw + rs + ops:
        cp.wait_send()
    for t in range(2):
        some = msg.at[t, pl.ds(0, CHIPS - 1)]
        pltpu.make_async_copy(some, some, a2a_s.at[t]).wait()


def hand_over(*refs):
    results, outs, wide, sem = refs[:5], refs[5:10], refs[10], refs[11]
    push = [pltpu.make_async_copy(results[i] if i < 4 else wide, outs[i], sem.at[i]) for i in range(5)]
    for i in (2, 3, 0, 1):
        push[i].start()
    scale = 1.0 / (N_GRAPH * YS * 256) ** 0.5
    for k in range(2):
        for h in range(2):
            wide[k, :, h * 128 : (h + 1) * 128] = (
                results[4][k, h * 16 : (h + 1) * 16].astype(F32).reshape(256, 128) * scale)
    push[4].start()
    for cp in push:
        cp.wait()


def shards(
    feats, w_self, w_neigh, block_vals, block_dst, block_src, block_count, prev_partial,
    mirror_rows, send_count, master_rows, momentum, cotangent, prev_grad, grad_momentum,
):
    sds = jax.ShapeDtypeStruct
    hbm = pl.BlockSpec(memory_space=pl.ANY)
    vm = pl.BlockSpec(memory_space=pltpu.VMEM)
    V, S = pltpu.VMEM, pltpu.SMEM
    dma = pltpu.SemaphoreType.DMA
    mat = lambda dt: V((256, 256), dt)
    results = pl.pallas_call(
        kernel,
        out_shape=(
            mat(BF), mat(BF), mat(F32), mat(F32), V((2, 32, 16, 128), BF),
        ),
        in_specs=[hbm] * 15,
        out_specs=[vm] * 5,
        scratch_shapes=[
            V((YS, 256, 256), BF), mat(BF), mat(BF), V((32, 128, 128), BF), mat(BF), mat(BF), mat(F32), mat(BF), mat(F32),
            V((4, N_GRAPH), I32), V((4, N_GRAPH), I32), V((1, N_GRAPH), I32), S((1, 32), I32), S((1, 32), I32), S((1, 1), I32),
            V((2, N_GRAPH * 8, 128), F32), V((2, CHIPS, 16, 128), BF), V((2, CHIPS, CORES, 16, 128), BF),
            V((YS, 256, 256), BF), V((YS, 256, 256), BF), V((YS, 256, 256), BF), V((YS, 256, 256), BF),
            V((32, 16, 128), BF), V((32, 16, 128), BF), V((32, 16, 128), BF), V((32, 16, 128), F32),
            V((XS * YS - 1, 2, 16, 128), BF), V((ZS, 2, 16, 128), BF),
            V((YS - 1, 256, 256), BF), V((YS - 1, 256, 256), BF),
            dma((15,)), dma((YS - 1,)), dma((YS - 1,)), dma((2,)), dma((2,)), dma((2,)), dma((2,)),
            dma((YS - 1,)), dma((YS - 1,)), dma((40,)), dma((40,)),
        ],
        compiler_params=pltpu.CompilerParams(
            collective_id=0, has_side_effects=True, vmem_limit_bytes=24 * 1024 * 1024),
    )(*[a if a.size == 1 else pltpu.with_memory_space_constraint(a, pltpu.HBM) for a in (
        feats[0, 0], w_self, w_neigh, block_vals[0, 0], block_dst[0], block_src[0], block_count,
        prev_partial[0, 0], jnp.swapaxes(mirror_rows[0, 0], 0, 1), send_count[0], jnp.swapaxes(master_rows[0, 0], 0, 1),
        momentum[0, 0], cotangent[0, 0], prev_grad[0, 0], grad_momentum[0, 0],
    )])
    hidden, fgrad, sp, sg, wg = pl.pallas_call(
        hand_over,
        out_shape=tuple(sds(r.shape, r.dtype) for r in results[:4]) + (sds((2, 256, 256), F32),),
        in_specs=[vm] * 5,
        out_specs=[hbm] * 5,
        scratch_shapes=[V((2, 256, 256), F32), dma((5,))],
        compiler_params=pltpu.CompilerParams(vmem_limit_bytes=24 * 1024 * 1024),
    )(*results)
    return hidden[None, None], fgrad[None, None], sp[None, None], sg[None, None], wg


def solution(mesh):
    gs = lambda n: P("graph", "slab", *([None] * n))
    in_specs = (
        gs(2), P(), P(), gs(3), gs(1), gs(1), gs(0), gs(2), gs(2), gs(1), gs(2), gs(2), gs(2), gs(2), gs(2),
    )
    out_specs = (gs(2), gs(2), gs(2), gs(2), P())
    return jax.shard_map(shards, mesh=mesh, in_specs=in_specs, out_specs=out_specs, check_vma=False)
```
